32 devices in a mesh: cuts: 16 (over z, y, core), coil: 2 (over x).
Axes of the slice: x: 2, y: 2, z: 4, core: 2. Of those that a mesh axis runs over, the one named last changes fastest.
Arguments:
- volume: bfloat16 [2, 256, 256, 256], P(None, 'cuts', 'coil'), may hold values from -6 to 6
- coil_maps: bfloat16 [16, 2, 256, 256, 256], P('coil', None, 'cuts'), may hold values from -3 to 3
- kspace: bfloat16 [16, 2, 256, 256, 256], P('coil', None, None, 'cuts'), may hold values from -3 to 3
- line_mask: int32 [256, 256], replicated, may hold values 0 or 1
Outputs:
- updated: bfloat16 [2, 256, 256, 256], P(None, 'coil', 'cuts')
The draws below stay inside these ranges and needn't reach their ends.
All inputs are finite; a program needn't handle non-finite values.
Results may differ from the reference program's by a relative error of at most 0.012.
Values may be sent and summed in bfloat16 or wider, within the bound.
No kernel may reach another device: no remote copies, remote signals or barrier semaphores. Data moves between devices by JAX's collectives and lax.ppermute only.
A program may use at most 384 MiB of HBM per device.

```python
import math
import jax
import jax.numpy as jnp
from jax import lax

EDGE = 256
COILS = 16


def touch_ends(drawn, rng, least, largest):
    spot = [jax.random.randint(jax.random.fold_in(rng, axis), (), 0, length) for axis, length in enumerate(drawn.shape)]
    widest = drawn.shape.index(max(drawn.shape))
    next_to = spot[:widest] + [(spot[widest] + 1) % drawn.shape[widest]] + spot[widest + 1:]
    return drawn.at[tuple(spot)].set(least).at[tuple(next_to)].set(largest)


def levels(key, shape, shards, smallest, high):
    def one(axis_at, parts):
        draws = jax.random.uniform(jax.random.fold_in(jax.random.fold_in(key, 6), axis_at), (parts,), jnp.float32, smallest / len(shards), high / len(shards))
        return jnp.repeat(jnp.exp(draws), shape[axis_at] // parts).reshape((-1,) + (1,) * (len(shape) - axis_at - 1))

    loudness = one(*shards[0])
    for cut in shards[1:]:
        loudness = loudness * one(*cut)
    return loudness


def bell_draw(stream_key, extent, width, limit, pieces=(), kind=jnp.bfloat16):
    entries = jax.random.normal(stream_key, extent, jnp.float32) * width
    if len(pieces) > 0:
        entries = levels(stream_key, extent, pieces, -0.22, 0.18) * entries
    return jnp.clip(entries, min=-limit, max=limit).astype(kind)


def setup_inputs(seed: int = 0) -> dict:
    splits = jax.random.split(jax.random.key(seed), 5)
    volume = bell_draw(splits[0], (2, EDGE, EDGE, EDGE), 1.0, 6.0, ((1, 16), (2, 2)))
    coil_maps = bell_draw(splits[1], (COILS, 2, EDGE, EDGE, EDGE), 0.5, 3.0, ((0, 2), (2, 16)))
    kspace = bell_draw(splits[2], (COILS, 2, EDGE, EDGE, EDGE), 0.5, 3.0, ((0, 2), (3, 16)))
    line_mask = touch_ends((jax.random.randint(splits[3], (EDGE, EDGE), 0, 2) < 1).astype(jnp.int32), jax.random.fold_in(splits[3], 1), 0, 1)
    return dict(volume=volume, coil_maps=coil_maps, kspace=kspace, line_mask=line_mask)


def tables(length):
    counter = jnp.arange(length, dtype=jnp.int32)
    product = counter[:, None] * counter[None, :] % length
    angles = product.astype(jnp.float32) * (2.0 * math.pi / length)
    factor = 1.0 / math.sqrt(length)
    return ((jnp.cos(angles) * factor).astype(jnp.bfloat16), (jnp.sin(angles) * factor).astype(jnp.bfloat16))

def contract(pattern, values, table):
    return jnp.einsum(pattern, values.astype(jnp.float32), table.astype(jnp.float32), precision=lax.Precision.HIGHEST)

def transform(real_part, imag_part, cos_table, sin_table, pattern, inverse):
    real_cos = contract(pattern, real_part, cos_table)
    real_sin = contract(pattern, real_part, sin_table)
    imag_cos = contract(pattern, imag_part, cos_table)
    imag_sin = contract(pattern, imag_part, sin_table)
    if inverse:
        return ((real_cos - imag_sin).astype(jnp.bfloat16), (imag_cos + real_sin).astype(jnp.bfloat16))
    return ((real_cos + imag_sin).astype(jnp.bfloat16), (imag_cos - real_sin).astype(jnp.bfloat16))

def reference(volume, coil_maps, kspace, line_mask):
    cos_table, sin_table = tables(EDGE)
    sampled = line_mask.astype(jnp.float32)
    vol_real = volume[0].astype(jnp.float32)
    vol_imag = volume[1].astype(jnp.float32)

    def one_coil(carry, pair):
        maps_one, data_one = pair
        map_real = maps_one[0].astype(jnp.float32)
        map_imag = maps_one[1].astype(jnp.float32)
        coil_real = (map_real * vol_real - map_imag * vol_imag).astype(jnp.bfloat16)
        coil_imag = (map_real * vol_imag + map_imag * vol_real).astype(jnp.bfloat16)
        z_real, z_imag = transform(coil_real, coil_imag, cos_table, sin_table, 'xyn,nk->xyk', False)
        k_real, k_imag = transform(z_real, z_imag, cos_table, sin_table, 'xnz,nk->xkz', False)
        h_real, h_imag = transform(data_one[0], data_one[1], cos_table, sin_table, 'nyz,nk->kyz', True)
        res_real = (sampled * (k_real.astype(jnp.float32) - h_real.astype(jnp.float32))).astype(jnp.bfloat16)
        res_imag = (sampled * (k_imag.astype(jnp.float32) - h_imag.astype(jnp.float32))).astype(jnp.bfloat16)
        y_real, y_imag = transform(res_real, res_imag, cos_table, sin_table, 'xnz,nk->xkz', True)
        b_real, b_imag = transform(y_real, y_imag, cos_table, sin_table, 'xyn,nk->xyk', True)
        back_real = b_real.astype(jnp.float32)
        back_imag = b_imag.astype(jnp.float32)
        grad_real = map_real * back_real + map_imag * back_imag
        grad_imag = map_real * back_imag - map_imag * back_real
        return (carry + jnp.stack([grad_real, grad_imag]), None)
    start = jnp.zeros((2, EDGE, EDGE, EDGE), jnp.float32)
    gradient, _ = lax.scan(one_coil, start, (coil_maps, kspace))
    return (volume.astype(jnp.float32) - 0.5 * gradient).astype(jnp.bfloat16)
```

```python
import functools
import math

import jax
import jax.numpy as jnp
from jax import lax
from jax.experimental import pallas as pl
from jax.experimental.pallas import tpu as pltpu
from jax.sharding import PartitionSpec as P

F32 = jnp.float32
BF16 = jnp.bfloat16
VMEM = 56 * 1024 * 1024


def tables(length):
    counter = jnp.arange(length, dtype=jnp.int32)
    product = counter[:, None] * counter[None, :] % length
    angles = product.astype(jnp.float32) * (2.0 * math.pi / length)
    factor = 1.0 / math.sqrt(length)
    return (
        (jnp.cos(angles) * factor).astype(jnp.bfloat16),
        (jnp.sin(angles) * factor).astype(jnp.bfloat16),
    )


def dot(a, b):
    return lax.dot_general(a, b, (((1,), (0,)), ((), ())), preferred_element_type=F32)


def cost(flops, bytes_accessed):
    return pl.CostEstimate(flops=int(flops), bytes_accessed=int(bytes_accessed), transcendentals=0)


def layout(line_mask, parts):
    edge = line_mask.shape[1]
    slab = line_mask.shape[0] // parts
    slots = edge // 2 * (slab + 1)
    half = edge // 2
    low = [max(half * k - (edge if k % 2 == 0 else half), 0) for k in range(slab)]
    high = [min(half * k + (edge if k % 2 == 0 else 3 * half), slots) for k in range(slab)]
    start_of_window = [min(at, slots - 2 * edge) for at in low]
    low, high, start_of_window = (jnp.array(v, jnp.int32) for v in (low, high, start_of_window))
    sampled = line_mask != 0
    upper = jnp.triu(jnp.ones((edge, edge), BF16), 1)
    rank = jnp.dot(sampled.astype(BF16), upper, preferred_element_type=F32).astype(jnp.int32)
    count = jnp.sum(sampled.astype(jnp.int32), axis=1).reshape(parts, slab)
    before = jnp.cumsum(count, axis=1) - count
    shift = lax.cummax(low[None, :] - before, axis=1)
    start = before + shift
    fits = jnp.all(start + count <= high[None, :])
    place = jnp.where(sampled, start.reshape(-1, 1) + rank, -1)
    window = jnp.tile(start_of_window, parts)[:, None]
    relative = jnp.where(sampled, place - window, -1)
    return fits, place, relative, slots


def compact_kernel(tiles, slots, k_ref, s_ref, t_ref, out_ref):
    slab, _, edge = k_ref.shape[1:]
    rows = out_ref.shape[2]
    parts = out_ref.shape[0]

    def tile(at, width):
        picked = None
        for j in range(4):
            k = jnp.clip(2 * at - 1 + j, 0, slab - 1)
            term = dot(k_ref[0, k], s_ref[at, j][:, :width])
            picked = term if picked is None else picked + term
        moved = dot(t_ref[...], picked.astype(BF16)).astype(BF16)
        return moved.reshape(parts, rows, width)

    @pl.loop(0, tiles)
    def _(at):
        out_ref[:, 0, :, pl.ds(pl.multiple_of(at * edge, edge), edge)] = tile(at, edge)

    rest = slots - tiles * edge
    if rest:
        out_ref[:, 0, :, tiles * edge :] = tile(tiles, rest)


def compact(data, select, table, parts, slots):
    coils, slab, both, edge = data.shape
    tiles = slots // edge
    rows = both // parts
    return pl.pallas_call(
        functools.partial(compact_kernel, tiles, slots),
        grid=(coils,),
        in_specs=[
            pl.BlockSpec((1, slab, both, edge), lambda c: (c, 0, 0, 0)),
            pl.BlockSpec(select.shape, lambda c: (0, 0, 0, 0)),
            pl.BlockSpec(table.shape, lambda c: (0, 0)),
        ],
        out_specs=pl.BlockSpec((parts, 1, rows, slots), lambda c: (0, c, 0, 0)),
        out_shape=jax.ShapeDtypeStruct((parts, coils, rows, slots), BF16),
        compiler_params=pltpu.CompilerParams(vmem_limit_bytes=VMEM),
        cost_estimate=cost(
            coils * 2 * slots * both * (4 * edge + both), 2 * coils * (data.size // coils + both * slots)
        ),
    )(data, select, table)


def expand_kernel(windows, rel_ref, in_ref, out_ref):
    edge = rel_ref.shape[1]
    rows = out_ref.shape[1]
    place = lax.broadcasted_iota(jnp.int32, (2 * edge, edge), 0)
    for k, at in enumerate(windows):
        chosen = jnp.where(place == rel_ref[k : k + 1, :], 1.0, 0.0).astype(BF16)
        source = in_ref[0, :, :, at : at + 2 * edge].reshape(rows, 2 * edge)
        out_ref[k] = dot(source, chosen).astype(BF16)


def expand(arrived, relative, windows):
    parts, coils, rows, slots = arrived.shape
    edge = relative.shape[1]
    slab = relative.shape[0] // parts
    return pl.pallas_call(
        functools.partial(expand_kernel, windows),
        grid=(parts,),
        in_specs=[
            pl.BlockSpec((slab, edge), lambda d: (d, 0)),
            pl.BlockSpec((1, coils, rows, slots), lambda d: (d, 0, 0, 0)),
        ],
        out_specs=pl.BlockSpec((slab, coils * rows, edge), lambda d: (d, 0, 0)),
        out_shape=jax.ShapeDtypeStruct((parts * slab, coils * rows, edge), BF16),
        compiler_params=pltpu.CompilerParams(vmem_limit_bytes=VMEM),
        cost_estimate=cost(
            parts * slab * coils * rows * edge * edge * 4, 2 * (arrived.size + parts * slab * coils * rows * edge)
        ),
    )(relative, arrived)


def forward_kernel(maps_ref, vol_ref, right_ref, left_ref, out_ref):
    edge = vol_ref.shape[3]
    for i in range(vol_ref.shape[1]):
        map_real, map_imag = maps_ref[0, 0, i].astype(F32), maps_ref[0, 1, i].astype(F32)
        vol_real, vol_imag = vol_ref[0, i].astype(F32), vol_ref[1, i].astype(F32)
        real = (map_real * vol_real - map_imag * vol_imag).astype(BF16)
        imag = (map_real * vol_imag + map_imag * vol_real).astype(BF16)
        along = dot(jnp.concatenate([real, imag], axis=1), right_ref[...]).astype(BF16)
        stacked = jnp.concatenate([along[:, :edge], along[:, edge:]], axis=0)
        out_ref[0, i] = dot(left_ref[...], stacked).astype(BF16)


def forward(maps, volume, right, left, group):
    coils, _, deep, edge, _ = maps.shape
    return pl.pallas_call(
        forward_kernel,
        grid=(deep // group, coils),
        in_specs=[
            pl.BlockSpec((1, 2, group, edge, edge), lambda x, c: (c, 0, x, 0, 0)),
            pl.BlockSpec((2, group, edge, edge), lambda x, c: (0, x, 0, 0)),
            pl.BlockSpec(right.shape, lambda x, c: (0, 0)),
            pl.BlockSpec(left.shape, lambda x, c: (0, 0)),
        ],
        out_specs=pl.BlockSpec((1, group, 2 * edge, edge), lambda x, c: (c, x, 0, 0)),
        out_shape=jax.ShapeDtypeStruct((coils, deep, 2 * edge, edge), BF16),
        compiler_params=pltpu.CompilerParams(vmem_limit_bytes=VMEM),
        cost_estimate=cost(coils * deep * edge**3 * 16, 4 * maps.size),
    )(maps, volume, right, left)


def backward_kernel(first, *refs):
    if first:
        maps_ref, k_ref, h_ref, mask_ref, left_ref, right_ref, out_ref = refs
    else:
        maps_ref, k_ref, h_ref, mask_ref, left_ref, right_ref, sum_ref, out_ref = refs
    edge = mask_ref.shape[1]
    sampled = mask_ref[...].astype(F32)
    sampled = jnp.concatenate([sampled, sampled], axis=0)

    @pl.when(pl.program_id(1) == 0)
    def _():
        out_ref[...] = jnp.zeros_like(out_ref) if first else sum_ref[...]

    for i in range(k_ref.shape[1]):
        hybrid = h_ref[0, :, i].reshape(2 * edge, edge)
        residual = (sampled * (k_ref[0, i].astype(F32) - hybrid.astype(F32))).astype(BF16)
        back = dot(left_ref[...], residual).astype(BF16)
        back = jnp.concatenate([back[:edge], back[edge:]], axis=1)
        back = dot(back, right_ref[...]).astype(BF16).astype(F32)
        real, imag = back[:, :edge], back[:, edge:]
        map_real, map_imag = maps_ref[0, 0, i].astype(F32), maps_ref[0, 1, i].astype(F32)
        out_ref[0, i] += map_real * real + map_imag * imag
        out_ref[1, i] += map_real * imag - map_imag * real


def backward(maps, coil_kspace, hybrid, line_mask, left, right, total, first_coil, group):
    coils, _, deep, edge, _ = hybrid.shape
    spec_sum = pl.BlockSpec((2, group, edge, edge), lambda x, c: (0, x, 0, 0))
    first = total is None
    return pl.pallas_call(
        functools.partial(backward_kernel, first),
        grid=(deep // group, coils),
        in_specs=[
            pl.BlockSpec((1, 2, group, edge, edge), lambda x, c: (first_coil + c, 0, x, 0, 0)),
            pl.BlockSpec((1, group, 2 * edge, edge), lambda x, c: (first_coil + c, x, 0, 0)),
            pl.BlockSpec((1, 2, group, edge, edge), lambda x, c: (c, 0, x, 0, 0)),
            pl.BlockSpec(line_mask.shape, lambda x, c: (0, 0)),
            pl.BlockSpec(left.shape, lambda x, c: (0, 0)),
            pl.BlockSpec(right.shape, lambda x, c: (0, 0)),
        ]
        + ([] if first else [spec_sum]),
        out_specs=spec_sum,
        out_shape=jax.ShapeDtypeStruct((2, deep, edge, edge), F32),
        compiler_params=pltpu.CompilerParams(vmem_limit_bytes=VMEM),
        cost_estimate=cost(coils * deep * edge**3 * 16, 6 * hybrid.size + 16 * deep * edge**2),
    )(maps, coil_kspace, hybrid, line_mask, left, right, *([] if first else [total]))


def body(coil_groups, volume, coil_maps, kspace, line_mask):
    coils, _, deep, edge, _ = coil_maps.shape
    slab = kspace.shape[3]
    parts = edge // slab
    me = lax.axis_index("cuts")
    cos_table, sin_table = tables(edge)
    turn = jnp.block([[cos_table, sin_table], [-sin_table, cos_table]])
    turn_back = jnp.block([[cos_table, -sin_table], [sin_table, cos_table]])
    by_destination = turn_back.reshape(2, parts, deep, 2 * edge).transpose(1, 0, 2, 3).reshape(2 * edge, 2 * edge)
    fits, place, relative, slots = layout(line_mask, parts)
    half = edge // 2
    windows = tuple(
        min(max(half * k - (edge if k % 2 == 0 else half), 0), slots - 2 * edge) for k in range(slab)
    )
    full_slab = lax.all_gather(volume, "coil", axis=2, tiled=True)
    chunks = min(4, coils)
    each = coils // chunks
    group = min(4, deep)

    def send_sampled(full_slab):
        mine = lax.dynamic_slice_in_dim(place, me * slab, slab, 0)
        tiles = -(-slots // edge)
        member = jnp.clip(2 * jnp.arange(tiles)[:, None] - 1 + jnp.arange(4)[None, :], -1, slab)
        padded = jnp.pad(mine, ((1, 1), (0, 0)), constant_values=-1)
        offset = padded[member + 1] - edge * jnp.arange(tiles)[:, None, None]
        select = (offset[..., None] == jnp.arange(edge)).astype(BF16)
        out = []
        for i in range(chunks):
            part = lax.slice_in_dim(kspace, i * each, (i + 1) * each, axis=0)
            data = part.transpose(0, 3, 1, 2, 4).reshape(each, slab, 2 * edge, edge)
            sent = compact(data, select, by_destination, parts, slots)
            out.append(lax.all_to_all(sent, "cuts", split_axis=0, concat_axis=0, tiled=True))
        coil_kspace = forward(coil_maps, full_slab, turn_back, turn, group)
        total = None
        for i in range(chunks):
            hybrid = expand(out[i], relative, windows)
            hybrid = hybrid.reshape(edge, each, 2, deep, edge).transpose(1, 2, 3, 0, 4)
            total = backward(
                coil_maps, coil_kspace, hybrid, line_mask, turn_back, turn, total, i * each, group
            )
        return total

    def send_all(full_slab):
        out = []
        for i in range(chunks):
            part = lax.slice_in_dim(kspace, i * each, (i + 1) * each, axis=0)
            data = part.transpose(0, 3, 1, 2, 4).reshape(each, slab, 2 * edge, edge)
            moved = jnp.einsum("xn,ckny->xcky", by_destination, data, preferred_element_type=F32).astype(BF16)
            moved = moved.reshape(parts, 2, deep, each, slab, edge)
            out.append(lax.all_to_all(moved, "cuts", split_axis=0, concat_axis=0, tiled=True))
        coil_kspace = forward(coil_maps, full_slab, turn_back, turn, group)
        total = None
        for i in range(chunks):
            hybrid = out[i].transpose(3, 1, 2, 0, 4, 5).reshape(each, 2, deep, edge, edge)
            total = backward(
                coil_maps, coil_kspace, hybrid, line_mask, turn_back, turn, total, i * each, group
            )
        return total

    total = lax.cond(fits, send_sampled, send_all, full_slab)
    return finish(coil_groups, full_slab, total)


def finish(coil_groups, full_slab, total):
    _, deep, edge, _ = total.shape
    mine = lax.axis_index("coil")
    share = deep // coil_groups
    summed = lax.dynamic_slice_in_dim(total, mine * share, share, 1)
    for step in range(1, coil_groups):
        other = lax.rem(mine + step, coil_groups)
        away = lax.dynamic_slice_in_dim(total, other * share, share, 1).astype(BF16)
        ring = [(i, (i + step) % coil_groups) for i in range(coil_groups)]
        summed = summed + lax.ppermute(away, "coil", ring).astype(F32)
    base = lax.dynamic_slice_in_dim(full_slab, mine * share, share, 1).astype(F32)
    updated = (base - 0.5 * summed).astype(BF16)
    updated = lax.all_to_all(updated, "cuts", split_axis=2, concat_axis=1, tiled=True)
    parts = edge // deep
    slab = updated.shape[2]
    updated = updated.reshape(2, coil_groups, parts // coil_groups, share, slab, edge)
    updated = lax.all_to_all(updated, "coil", split_axis=1, concat_axis=1, tiled=True)
    updated = updated.transpose(0, 2, 1, 3, 4, 5)
    return updated.reshape(2, edge // coil_groups, slab, edge)


def solution(mesh):
    placed = (
        P(None, "cuts", "coil", None),
        P("coil", None, "cuts", None, None),
        P("coil", None, None, "cuts", None),
        P(),
    )
    return jax.shard_map(
        functools.partial(body, mesh.shape["coil"]),
        mesh=mesh,
        in_specs=placed,
        out_specs=P(None, "coil", "cuts", None),
        check_vma=False,
    )
```

```python
import functools
import math

import jax
import jax.numpy as jnp
from jax import lax
from jax.experimental import pallas as pl
from jax.experimental.pallas import tpu as pltpu
from jax.sharding import PartitionSpec as P

F32 = jnp.float32
BF16 = jnp.bfloat16
VMEM = 56 * 1024 * 1024


def tables(length):
    counter = jnp.arange(length, dtype=jnp.int32)
    product = counter[:, None] * counter[None, :] % length
    angles = product.astype(jnp.float32) * (2.0 * math.pi / length)
    factor = 1.0 / math.sqrt(length)
    return (
        (jnp.cos(angles) * factor).astype(jnp.bfloat16),
        (jnp.sin(angles) * factor).astype(jnp.bfloat16),
    )


def dot(a, b):
    return lax.dot_general(a, b, (((1,), (0,)), ((), ())), preferred_element_type=F32)


def cost(flops, bytes_accessed):
    return pl.CostEstimate(flops=int(flops), bytes_accessed=int(bytes_accessed), transcendentals=0)


def layout(line_mask, parts):
    edge = line_mask.shape[1]
    slab = line_mask.shape[0] // parts
    slots = edge // 2 * (slab + 1)
    half = edge // 2
    low = [max(half * k - (edge if k % 2 == 0 else half), 0) for k in range(slab)]
    high = [min(half * k + (edge if k % 2 == 0 else 3 * half), slots) for k in range(slab)]
    start_of_window = [min(at, slots - 2 * edge) for at in low]
    low, high, start_of_window = (jnp.array(v, jnp.int32) for v in (low, high, start_of_window))
    sampled = line_mask != 0
    upper = jnp.triu(jnp.ones((edge, edge), BF16), 1)
    rank = jnp.dot(sampled.astype(BF16), upper, preferred_element_type=F32).astype(jnp.int32)
    count = jnp.sum(sampled.astype(jnp.int32), axis=1).reshape(parts, slab)
    before = jnp.cumsum(count, axis=1) - count
    shift = lax.cummax(low[None, :] - before, axis=1)
    start = before + shift
    fits = jnp.all(start + count <= high[None, :])
    place = jnp.where(sampled, start.reshape(-1, 1) + rank, -1)
    window = jnp.tile(start_of_window, parts)[:, None]
    relative = jnp.where(sampled, place - window, -1)
    return fits, place, relative, slots


def compact_kernel(tiles, slots, k_ref, s_ref, t_ref, out_ref, lines_ref):
    slab, _, edge = lines_ref.shape
    rows = out_ref.shape[2]
    parts = out_ref.shape[0]
    step = 32

    @pl.loop(0, edge // step)
    def _(at):
        first = pl.multiple_of(at * step, step)
        for r in range(2):
            block = jnp.swapaxes(k_ref[0, r, pl.ds(first, step)], 0, 1)
            lines_ref[:, pl.ds(pl.multiple_of(r * edge + first, step), step), :] = block

    def tile(at, width):
        picked = None
        for j in range(4):
            k = jnp.clip(2 * at - 1 + j, 0, slab - 1)
            term = dot(lines_ref[k], s_ref[at, j][:, :width])
            picked = term if picked is None else picked + term
        moved = dot(t_ref[...], picked.astype(BF16)).astype(BF16)
        return moved.reshape(parts, rows, width)

    @pl.loop(0, tiles)
    def _(at):
        out_ref[:, 0, :, pl.ds(pl.multiple_of(at * edge, edge), edge)] = tile(at, edge)

    rest = slots - tiles * edge
    if rest:
        out_ref[:, 0, :, tiles * edge :] = tile(tiles, rest)


def compact(data, first_coil, coils, select, table, parts, slots):
    _, _, edge, slab, _ = data.shape
    tiles = slots // edge
    rows = 2 * edge // parts
    return pl.pallas_call(
        functools.partial(compact_kernel, tiles, slots),
        grid=(coils,),
        in_specs=[
            pl.BlockSpec((1, 2, edge, slab, edge), lambda c: (first_coil + c, 0, 0, 0, 0)),
            pl.BlockSpec(select.shape, lambda c: (0, 0, 0, 0)),
            pl.BlockSpec(table.shape, lambda c: (0, 0)),
        ],
        out_specs=pl.BlockSpec((parts, 1, rows, slots), lambda c: (0, c, 0, 0)),
        out_shape=jax.ShapeDtypeStruct((parts, coils, rows, slots), BF16),
        scratch_shapes=[pltpu.VMEM((slab, 2 * edge, edge), BF16)],
        compiler_params=pltpu.CompilerParams(vmem_limit_bytes=VMEM),
        cost_estimate=cost(
            coils * 4 * slots * edge * 6 * edge, 4 * coils * edge * (slab * edge + slots)
        ),
    )(data, select, table)


def expand_kernel(windows, rel_ref, in_ref, out_ref, lines_ref):
    edge = rel_ref.shape[1]
    slab, rows, _ = lines_ref.shape
    place = lax.broadcasted_iota(jnp.int32, (2 * edge, edge), 0)
    for k, at in enumerate(windows):
        chosen = jnp.where(place == rel_ref[k : k + 1, :], 1.0, 0.0).astype(BF16)
        source = in_ref[0, :, :, at : at + 2 * edge].reshape(rows, 2 * edge)
        lines_ref[k] = dot(source, chosen).astype(BF16)
    for at in range(0, rows, 16):
        out_ref[at : at + 16] = jnp.swapaxes(lines_ref[:, at : at + 16, :], 0, 1)


def expand(arrived, relative, windows):
    parts, coils, rows, slots = arrived.shape
    edge = relative.shape[1]
    slab = relative.shape[0] // parts
    rows = coils * rows
    return pl.pallas_call(
        functools.partial(expand_kernel, windows),
        grid=(parts,),
        in_specs=[
            pl.BlockSpec((slab, edge), lambda d: (d, 0)),
            pl.BlockSpec((1,) + arrived.shape[1:], lambda d: (d, 0, 0, 0)),
        ],
        out_specs=pl.BlockSpec((rows, slab, edge), lambda d: (0, d, 0)),
        out_shape=jax.ShapeDtypeStruct((rows, parts * slab, edge), BF16),
        scratch_shapes=[pltpu.VMEM((slab, rows, edge), BF16)],
        compiler_params=pltpu.CompilerParams(vmem_limit_bytes=VMEM),
        cost_estimate=cost(parts * slab * rows * edge * edge * 4, 2 * (arrived.size + parts * slab * rows * edge)),
    )(relative, arrived)


def forward_kernel(maps_ref, vol_ref, right_ref, left_ref, out_ref):
    edge = vol_ref.shape[3]
    for i in range(vol_ref.shape[1]):
        map_real, map_imag = maps_ref[0, 0, i].astype(F32), maps_ref[0, 1, i].astype(F32)
        vol_real, vol_imag = vol_ref[0, i].astype(F32), vol_ref[1, i].astype(F32)
        real = (map_real * vol_real - map_imag * vol_imag).astype(BF16)
        imag = (map_real * vol_imag + map_imag * vol_real).astype(BF16)
        along = dot(jnp.concatenate([real, imag], axis=1), right_ref[...]).astype(BF16)
        stacked = jnp.concatenate([along[:, :edge], along[:, edge:]], axis=0)
        out_ref[0, i] = dot(left_ref[...], stacked).astype(BF16)


def forward(maps, volume, right, left, group):
    coils, _, deep, edge, _ = maps.shape
    return pl.pallas_call(
        forward_kernel,
        grid=(deep // group, coils),
        in_specs=[
            pl.BlockSpec((1, 2, group, edge, edge), lambda x, c: (c, 0, x, 0, 0)),
            pl.BlockSpec((2, group, edge, edge), lambda x, c: (0, x, 0, 0)),
            pl.BlockSpec(right.shape, lambda x, c: (0, 0)),
            pl.BlockSpec(left.shape, lambda x, c: (0, 0)),
        ],
        out_specs=pl.BlockSpec((1, group, 2 * edge, edge), lambda x, c: (c, x, 0, 0)),
        out_shape=jax.ShapeDtypeStruct((coils, deep, 2 * edge, edge), BF16),
        compiler_params=pltpu.CompilerParams(vmem_limit_bytes=VMEM),
        cost_estimate=cost(coils * deep * edge**3 * 16, 4 * maps.size),
    )(maps, volume, right, left)


def backward_kernel(first, at_ref, *refs):
    if first:
        maps_ref, k_ref, h_ref, mask_ref, left_ref, right_ref, out_ref, sum_ref = refs
    else:
        maps_ref, k_ref, h_ref, mask_ref, left_ref, right_ref, before_ref, out_ref, sum_ref = refs
    edge = mask_ref.shape[1]
    sampled = mask_ref[...].astype(F32)
    sampled = jnp.concatenate([sampled, sampled], axis=0)

    @pl.when(pl.program_id(1) == 0)
    def _():
        sum_ref[...] = jnp.zeros_like(sum_ref) if first else before_ref[...]

    for i in range(k_ref.shape[1]):
        hybrid = h_ref[0, :, i].reshape(2 * edge, edge)
        residual = (sampled * (k_ref[0, i].astype(F32) - hybrid.astype(F32))).astype(BF16)
        back = dot(left_ref[...], residual).astype(BF16)
        back = jnp.concatenate([back[:edge], back[edge:]], axis=1)
        back = dot(back, right_ref[...]).astype(BF16).astype(F32)
        real, imag = back[:, :edge], back[:, edge:]
        map_real, map_imag = maps_ref[0, 0, i].astype(F32), maps_ref[0, 1, i].astype(F32)
        sum_ref[0, i] += map_real * real + map_imag * imag
        sum_ref[1, i] += map_real * imag - map_imag * real

    @pl.when(pl.program_id(1) == pl.num_programs(1) - 1)
    def _():
        out_ref[...] = sum_ref[...].astype(out_ref.dtype)


def backward(maps, coil_kspace, hybrid, line_mask, left, right, before, first_coil, first_x, count, group, kind):
    coils, _, _, edge, _ = hybrid.shape
    group = min(group, count)
    first = before is None
    block = (2, group, edge, edge)
    spec = pltpu.PrefetchScalarGridSpec(
        num_scalar_prefetch=1,
        grid=(count // group, coils),
        in_specs=[
            pl.BlockSpec((1, 2, group, edge, edge), lambda x, c, at: (first_coil + c, 0, at[0] + x, 0, 0)),
            pl.BlockSpec((1, group, 2 * edge, edge), lambda x, c, at: (first_coil + c, at[0] + x, 0, 0)),
            pl.BlockSpec((1, 2, group, edge, edge), lambda x, c, at: (c, 0, at[0] + x, 0, 0)),
            pl.BlockSpec(line_mask.shape, lambda x, c, at: (0, 0)),
            pl.BlockSpec(left.shape, lambda x, c, at: (0, 0)),
            pl.BlockSpec(right.shape, lambda x, c, at: (0, 0)),
        ]
        + ([] if first else [pl.BlockSpec(block, lambda x, c, at: (0, at[0] + x, 0, 0))]),
        out_specs=pl.BlockSpec(block, lambda x, c, at: (0, x, 0, 0)),
        scratch_shapes=[pltpu.VMEM(block, F32)],
    )
    start = jnp.full((1,), first_x // group, jnp.int32)
    return pl.pallas_call(
        functools.partial(backward_kernel, first),
        grid_spec=spec,
        out_shape=jax.ShapeDtypeStruct((2, count, edge, edge), kind),
        compiler_params=pltpu.CompilerParams(vmem_limit_bytes=VMEM),
        cost_estimate=cost(coils * count * edge**3 * 16, count * edge**2 * (12 * coils + 16)),
    )(start, maps, coil_kspace, hybrid, line_mask, left, right, *([] if first else [before]))


def body(coil_groups, volume, coil_maps, kspace, line_mask):
    coils, _, deep, edge, _ = coil_maps.shape
    slab = kspace.shape[3]
    parts = edge // slab
    me = lax.axis_index("cuts")
    mine = lax.axis_index("coil")
    cos_table, sin_table = tables(edge)
    turn = jnp.block([[cos_table, sin_table], [-sin_table, cos_table]])
    turn_back = jnp.block([[cos_table, -sin_table], [sin_table, cos_table]])
    by_destination = turn_back.reshape(2, parts, deep, 2 * edge).transpose(1, 0, 2, 3).reshape(2 * edge, 2 * edge)
    fits, place, relative, slots = layout(line_mask, parts)
    half = edge // 2
    windows = tuple(
        min(max(half * k - (edge if k % 2 == 0 else half), 0), slots - 2 * edge) for k in range(slab)
    )
    if coils % 2 == 0 and coils > 2:
        sizes = [1] + [2] * (coils // 2 - 1) + [1]
    else:
        sizes = [1] * coils
    firsts = [sum(sizes[:i]) for i in range(len(sizes))]
    group = min(4, deep)

    def step(pack, unpack):
        arrived = [exchange(pack(0))]
        full_slab = lax.all_gather(volume, "coil", axis=2, tiled=True)
        coil_kspace = forward(coil_maps, full_slab, turn_back, turn, group)
        total = None
        for i in range(1, len(sizes) + 1):
            if i < len(sizes):
                sent = pack(i)
                if i == 2:
                    sent, coil_kspace = lax.optimization_barrier((sent, coil_kspace))
                elif i > 2:
                    sent, total = lax.optimization_barrier((sent, total))
                arrived.append(exchange(sent))
            hybrid = unpack(i - 1, arrived[i - 1])
            at = functools.partial(
                backward, coil_maps, coil_kspace, hybrid, line_mask, turn_back, turn, total, firsts[i - 1]
            )
            if i < len(sizes):
                total = at(0, deep, group, F32)
        return finish(coil_groups, mine, full_slab, at, deep)

    def exchange(sent):
        return lax.all_to_all(sent, "cuts", split_axis=0, concat_axis=0, tiled=True)

    def send_sampled():
        own = lax.dynamic_slice_in_dim(place, me * slab, slab, 0)
        tiles = -(-slots // edge)
        member = jnp.clip(2 * jnp.arange(tiles)[:, None] - 1 + jnp.arange(4)[None, :], -1, slab)
        padded = jnp.pad(own, ((1, 1), (0, 0)), constant_values=-1)
        offset = padded[member + 1] - edge * jnp.arange(tiles)[:, None, None]
        select = (offset[..., None] == jnp.arange(edge)).astype(BF16)

        def pack(i):
            return compact(kspace, firsts[i], sizes[i], select, by_destination, parts, slots)

        def unpack(i, arrived):
            return expand(arrived, relative, windows).reshape(sizes[i], 2, deep, edge, edge)

        return step(pack, unpack)

    def send_all():
        def pack(i):
            part = lax.slice_in_dim(kspace, firsts[i], firsts[i] + sizes[i], axis=0)
            data = part.transpose(0, 3, 1, 2, 4).reshape(sizes[i], slab, 2 * edge, edge)
            moved = jnp.einsum("xn,ckny->xcky", by_destination, data, preferred_element_type=F32).astype(BF16)
            return moved.reshape(parts, 2, deep, sizes[i], slab, edge)

        def unpack(i, arrived):
            return arrived.transpose(3, 1, 2, 0, 4, 5).reshape(sizes[i], 2, deep, edge, edge)

        return step(pack, unpack)

    return lax.cond(fits, send_sampled, send_all)


def finish(coil_groups, mine, full_slab, gradient, deep):
    edge = full_slab.shape[2]
    parts = edge // deep
    pieces = min(2, deep // coil_groups)
    share = deep // coil_groups // pieces
    rings = [[(i, (i + s) % coil_groups) for i in range(coil_groups)] for s in range(coil_groups)]
    away = [
        [
            lax.ppermute(
                gradient((p * coil_groups + lax.rem(mine + s, coil_groups)) * share, share, share, BF16), "coil", rings[s]
            )
            for s in range(1, coil_groups)
        ]
        for p in range(pieces)
    ]
    out = []
    for p in range(pieces):
        at = (p * coil_groups + mine) * share
        summed = gradient(at, share, share, F32)
        for term in away[p]:
            summed = summed + term.astype(F32)
        base = lax.dynamic_slice_in_dim(full_slab, at, share, 1).astype(F32)
        updated = (base - 0.5 * summed).astype(BF16)
        updated = lax.all_to_all(updated, "cuts", split_axis=2, concat_axis=1, tiled=True)
        slab = updated.shape[2]
        updated = updated.reshape(2, coil_groups, parts // coil_groups, share, slab, edge)
        whole = jnp.zeros((2, parts // coil_groups, coil_groups, share, slab, edge), BF16)
        for s in range(coil_groups):
            to = lax.rem(mine + s, coil_groups)
            source = lax.rem(mine + coil_groups - s, coil_groups)
            moved = lax.dynamic_index_in_dim(updated, to, 1, keepdims=False)
            if s:
                moved = lax.ppermute(moved, "coil", rings[s])
            whole = lax.dynamic_update_index_in_dim(whole, moved[:, :, None], source, 2)
        out.append(whole)
    out = jnp.stack(out, axis=2)
    return out.reshape(2, edge // coil_groups, slab, edge)


def solution(mesh):
    placed = (
        P(None, "cuts", "coil", None),
        P("coil", None, "cuts", None, None),
        P("coil", None, None, "cuts", None),
        P(),
    )
    return jax.shard_map(
        functools.partial(body, mesh.shape["coil"]),
        mesh=mesh,
        in_specs=placed,
        out_specs=P(None, "coil", "cuts", None),
        check_vma=False,
    )
```

```python
import functools
import math

import jax
import jax.numpy as jnp
from jax import lax
from jax.experimental import pallas as pl
from jax.experimental.pallas import tpu as pltpu
from jax.sharding import PartitionSpec as P

F32 = jnp.float32
BF16 = jnp.bfloat16
VMEM = 56 * 1024 * 1024


def tables(length):
    counter = jnp.arange(length, dtype=jnp.int32)
    product = counter[:, None] * counter[None, :] % length
    angles = product.astype(jnp.float32) * (2.0 * math.pi / length)
    factor = 1.0 / math.sqrt(length)
    return (
        (jnp.cos(angles) * factor).astype(jnp.bfloat16),
        (jnp.sin(angles) * factor).astype(jnp.bfloat16),
    )


def dot(a, b):
    return lax.dot_general(a, b, (((1,), (0,)), ((), ())), preferred_element_type=F32)


def cost(flops, bytes_accessed):
    return pl.CostEstimate(flops=int(flops), bytes_accessed=int(bytes_accessed), transcendentals=0)


def layout(line_mask, parts):
    edge = line_mask.shape[1]
    slab = line_mask.shape[0] // parts
    half = edge // 2
    sampled = line_mask != 0
    upper = jnp.triu(jnp.ones((edge, edge), BF16), 1)
    rank = jnp.dot(sampled.astype(BF16), upper, preferred_element_type=F32).astype(jnp.int32)
    over = jnp.maximum(jnp.sum(sampled.astype(jnp.int32), axis=1).reshape(parts, slab) - half, 0)
    fits = jnp.all(jnp.sum(over, axis=1) <= half)
    before = (jnp.cumsum(over, axis=1) - over).reshape(-1, 1)
    place = jnp.where(sampled, rank + jnp.where(rank < half, 0, before), -1)
    return fits, place, half * (slab + 1)


def compact_kernel(pieces, k_ref, s_ref, t_ref, *refs):
    out_refs, lines_ref, over_ref = refs[:pieces], refs[pieces], refs[pieces + 1]
    slab, _, edge = lines_ref.shape
    half = edge // 2
    parts, _, rows, _ = out_refs[0].shape
    step = 32

    @pl.loop(0, edge // step)
    def _(at):
        first = pl.multiple_of(at * step, step)
        for r in range(2):
            block = jnp.swapaxes(k_ref[0, r, pl.ds(first, step)], 0, 1)
            lines_ref[:, pl.ds(pl.multiple_of(r * edge + first, step), step), :] = block

    def send(picked, places):
        moved = dot(t_ref[...], picked.astype(BF16)).astype(BF16)
        moved = moved.reshape(parts, pieces, rows, picked.shape[1])
        for p in range(pieces):
            out_refs[p][:, 0, :, places] = moved[:, p]

    over_ref[...] = jnp.zeros_like(over_ref)

    @pl.loop(0, slab // 2)
    def _(pair):
        one = dot(lines_ref[2 * pair], s_ref[2 * pair])
        two = dot(lines_ref[2 * pair + 1], s_ref[2 * pair + 1])
        over_ref[...] += one[:, half:] + two[:, half:]
        own = jnp.concatenate([one[:, :half], two[:, :half]], axis=1)
        send(own, pl.ds(pl.multiple_of(pair * edge, edge), edge))

    send(over_ref[...], pl.ds(slab * half, half))


def by_destination(table, parts, pieces):
    size = table.shape[0]
    rows = table.reshape(2, parts, pieces, size // (2 * parts * pieces), size)
    return rows.transpose(1, 2, 0, 3, 4).reshape(size, size)


def compact(data, first_coil, coils, pieces, select, table, parts, slots):
    _, _, edge, slab, _ = data.shape
    rows = 2 * edge // parts // pieces
    return pl.pallas_call(
        functools.partial(compact_kernel, pieces),
        grid=(coils,),
        in_specs=[
            pl.BlockSpec((1, 2, edge, slab, edge), lambda c: (first_coil + c, 0, 0, 0, 0)),
            pl.BlockSpec(select.shape, lambda c: (0, 0, 0)),
            pl.BlockSpec(table.shape, lambda c: (0, 0)),
        ],
        out_specs=[pl.BlockSpec((parts, 1, rows, slots), lambda c: (0, c, 0, 0))] * pieces,
        out_shape=[jax.ShapeDtypeStruct((parts, coils, rows, slots), BF16)] * pieces,
        scratch_shapes=[pltpu.VMEM((slab, 2 * edge, edge), BF16), pltpu.VMEM((2 * edge, edge // 2), F32)],
        compiler_params=pltpu.CompilerParams(vmem_limit_bytes=VMEM),
        cost_estimate=cost(coils * 4 * slots * edge * 4 * edge, 4 * coils * edge * (slab * edge + slots)),
    )(data, select, by_destination(table, parts, pieces))


def expand_kernel(place_ref, in_ref, out_ref, lines_ref):
    edge = place_ref.shape[1]
    half = edge // 2
    slab, rows, _ = lines_ref.shape
    places = lax.broadcasted_iota(jnp.int32, (edge, edge), 0)
    shared = in_ref[0, :, :, slab * half :].reshape(rows, half)
    for k in range(slab):
        chosen = jnp.where(places == place_ref[k : k + 1, :], 1.0, 0.0).astype(BF16)
        own = in_ref[0, :, :, k * half : (k + 1) * half].reshape(rows, half)
        lines_ref[k] = dot(jnp.concatenate([own, shared], axis=1), chosen).astype(BF16)
    for at in range(0, rows, 16):
        out_ref[at : at + 16] = jnp.swapaxes(lines_ref[:, at : at + 16, :], 0, 1)


def expand(arrived, place):
    parts, coils, rows, slots = arrived.shape
    edge = place.shape[1]
    slab = place.shape[0] // parts
    rows = coils * rows
    return pl.pallas_call(
        expand_kernel,
        grid=(parts,),
        in_specs=[
            pl.BlockSpec((slab, edge), lambda d: (d, 0)),
            pl.BlockSpec((1,) + arrived.shape[1:], lambda d: (d, 0, 0, 0)),
        ],
        out_specs=pl.BlockSpec((rows, slab, edge), lambda d: (0, d, 0)),
        out_shape=jax.ShapeDtypeStruct((rows, parts * slab, edge), BF16),
        scratch_shapes=[pltpu.VMEM((slab, rows, edge), BF16)],
        compiler_params=pltpu.CompilerParams(vmem_limit_bytes=VMEM),
        cost_estimate=cost(parts * slab * rows * edge * edge * 2, 2 * (arrived.size + parts * slab * rows * edge)),
    )(place, arrived)


def forward_kernel(maps_ref, vol_ref, right_ref, left_ref, out_ref):
    edge = vol_ref.shape[3]
    for i in range(vol_ref.shape[1]):
        map_real, map_imag = maps_ref[0, 0, i].astype(F32), maps_ref[0, 1, i].astype(F32)
        vol_real, vol_imag = vol_ref[0, i].astype(F32), vol_ref[1, i].astype(F32)
        real = (map_real * vol_real - map_imag * vol_imag).astype(BF16)
        imag = (map_real * vol_imag + map_imag * vol_real).astype(BF16)
        along = dot(jnp.concatenate([real, imag], axis=1), right_ref[...]).astype(BF16)
        stacked = jnp.concatenate([along[:, :edge], along[:, edge:]], axis=0)
        out_ref[0, i] = dot(left_ref[...], stacked).astype(BF16)


def forward(maps, volume, right, left, group):
    coils, _, deep, edge, _ = maps.shape
    return pl.pallas_call(
        forward_kernel,
        grid=(deep // group, coils),
        in_specs=[
            pl.BlockSpec((1, 2, group, edge, edge), lambda x, c: (c, 0, x, 0, 0)),
            pl.BlockSpec((2, group, edge, edge), lambda x, c: (0, x, 0, 0)),
            pl.BlockSpec(right.shape, lambda x, c: (0, 0)),
            pl.BlockSpec(left.shape, lambda x, c: (0, 0)),
        ],
        out_specs=pl.BlockSpec((1, group, 2 * edge, edge), lambda x, c: (c, x, 0, 0)),
        out_shape=jax.ShapeDtypeStruct((coils, deep, 2 * edge, edge), BF16),
        compiler_params=pltpu.CompilerParams(vmem_limit_bytes=VMEM),
        cost_estimate=cost(coils * deep * edge**3 * 16, 4 * maps.size),
    )(maps, volume, right, left)


def backward_kernel(first, at_ref, *refs):
    if first:
        maps_ref, k_ref, h_ref, mask_ref, left_ref, right_ref, out_ref, sum_ref = refs
    else:
        maps_ref, k_ref, h_ref, mask_ref, left_ref, right_ref, before_ref, out_ref, sum_ref = refs
    edge = mask_ref.shape[1]
    sampled = mask_ref[...].astype(F32)
    sampled = jnp.concatenate([sampled, sampled], axis=0)

    @pl.when(pl.program_id(1) == 0)
    def _():
        sum_ref[...] = jnp.zeros_like(sum_ref) if first else before_ref[...]

    for i in range(k_ref.shape[1]):
        hybrid = h_ref[0, :, i].reshape(2 * edge, edge)
        residual = (sampled * (k_ref[0, i].astype(F32) - hybrid.astype(F32))).astype(BF16)
        back = dot(left_ref[...], residual).astype(BF16)
        back = jnp.concatenate([back[:edge], back[edge:]], axis=1)
        back = dot(back, right_ref[...]).astype(BF16).astype(F32)
        real, imag = back[:, :edge], back[:, edge:]
        map_real, map_imag = maps_ref[0, 0, i].astype(F32), maps_ref[0, 1, i].astype(F32)
        sum_ref[0, i] += map_real * real + map_imag * imag
        sum_ref[1, i] += map_real * imag - map_imag * real

    @pl.when(pl.program_id(1) == pl.num_programs(1) - 1)
    def _():
        out_ref[...] = sum_ref[...].astype(out_ref.dtype)


def backward(
    maps, coil_kspace, line_mask, left, right, group, hybrid, hybrid_x, before, first_coil, first_x, count, kind
):
    coils, _, _, edge, _ = hybrid.shape
    group = min(group, count)
    first = before is None
    block = (2, group, edge, edge)
    spec = pltpu.PrefetchScalarGridSpec(
        num_scalar_prefetch=1,
        grid=(count // group, coils),
        in_specs=[
            pl.BlockSpec((1, 2, group, edge, edge), lambda x, c, at: (first_coil + c, 0, at[0] + x, 0, 0)),
            pl.BlockSpec((1, group, 2 * edge, edge), lambda x, c, at: (first_coil + c, at[0] + x, 0, 0)),
            pl.BlockSpec((1, 2, group, edge, edge), lambda x, c, at: (c, 0, at[0] + x - hybrid_x // group, 0, 0)),
            pl.BlockSpec(line_mask.shape, lambda x, c, at: (0, 0)),
            pl.BlockSpec(left.shape, lambda x, c, at: (0, 0)),
            pl.BlockSpec(right.shape, lambda x, c, at: (0, 0)),
        ]
        + ([] if first else [pl.BlockSpec(block, lambda x, c, at: (0, at[0] + x, 0, 0))]),
        out_specs=pl.BlockSpec(block, lambda x, c, at: (0, x, 0, 0)),
        scratch_shapes=[pltpu.VMEM(block, F32)],
    )
    start = jnp.full((1,), first_x // group, jnp.int32)
    return pl.pallas_call(
        functools.partial(backward_kernel, first),
        grid_spec=spec,
        out_shape=jax.ShapeDtypeStruct((2, count, edge, edge), kind),
        compiler_params=pltpu.CompilerParams(vmem_limit_bytes=VMEM),
        cost_estimate=cost(coils * count * edge**3 * 16, count * edge**2 * (12 * coils + 16)),
    )(start, maps, coil_kspace, hybrid, line_mask, left, right, *([] if first else [before]))


def body(coil_groups, volume, coil_maps, kspace, line_mask):
    coils, _, deep, edge, _ = coil_maps.shape
    slab = kspace.shape[3]
    parts = edge // slab
    me = lax.axis_index("cuts")
    mine = lax.axis_index("coil")
    cos_table, sin_table = tables(edge)
    turn = jnp.block([[cos_table, sin_table], [-sin_table, cos_table]])
    turn_back = jnp.block([[cos_table, -sin_table], [sin_table, cos_table]])
    fits, place, slots = layout(line_mask, parts)
    if coils >= 6:
        sizes = [1, (coils - 3) // 2, (coils - 2) // 2, 2]
    else:
        sizes = [1] * coils
    firsts = [sum(sizes[:i]) for i in range(len(sizes))]
    pieces = min(2, deep // coil_groups)
    planes = deep // pieces
    last = len(sizes) - 1
    group = min(4, deep)

    def step(pack, unpack):
        full_slab = lax.all_gather(volume, "coil", axis=2, tiled=True)
        arrived = []
        total = coil_kspace = None
        for i in range(last):
            (sent,) = pack(i, 1)
            if i == 1:
                sent, full_slab = lax.optimization_barrier((sent, full_slab))
                coil_kspace = forward(coil_maps, full_slab, turn_back, turn, group)
            elif i == 2:
                sent, coil_kspace = lax.optimization_barrier((sent, coil_kspace))
            arrived.append(exchange(sent))
        if coil_kspace is None:
            coil_kspace = forward(coil_maps, full_slab, turn_back, turn, group)
        back = functools.partial(backward, coil_maps, coil_kspace, line_mask, turn_back, turn, group)
        sent = list(pack(last, pieces))
        for i in range(last):
            if i == last - 1 and total is not None:
                sent[0], total = lax.optimization_barrier((sent[0], total))
            total = back(unpack(i, deep, arrived[i]), 0, total, firsts[i], 0, deep, F32)
        if pieces > 1:
            sent[1], total = lax.optimization_barrier((sent[1], total))
        arrived = [exchange(one) for one in sent]

        def gradient(p):
            hybrid = unpack(last, planes, arrived[p])

            def planes_from(first_x, count, kind, earlier=None):
                before = total
                if earlier is not None:
                    _, before = lax.optimization_barrier((earlier, total))
                return back(hybrid, p * planes, before, firsts[last], first_x, count, kind)

            return planes_from

        return finish(coil_groups, mine, full_slab, gradient, arrived, deep)

    def exchange(sent):
        return lax.all_to_all(sent, "cuts", split_axis=0, concat_axis=0, tiled=True)

    def send_sampled():
        own = lax.dynamic_slice_in_dim(place, me * slab, slab, 0)
        select = (own[..., None] == jnp.arange(edge)).astype(BF16)

        def pack(i, pieces):
            return compact(kspace, firsts[i], sizes[i], pieces, select, turn_back, parts, slots)

        def unpack(i, planes, arrived):
            return expand(arrived, place).reshape(sizes[i], 2, planes, edge, edge)

        return step(pack, unpack)

    def send_all():
        def pack(i, pieces):
            part = lax.slice_in_dim(kspace, firsts[i], firsts[i] + sizes[i], axis=0)
            data = part.transpose(0, 3, 1, 2, 4).reshape(sizes[i], slab, 2 * edge, edge)
            table = by_destination(turn_back, parts, pieces)
            moved = jnp.einsum("xn,ckny->xcky", table, data, preferred_element_type=F32).astype(BF16)
            moved = moved.reshape(parts, pieces, 2, deep // pieces, sizes[i], slab, edge)
            return [moved[:, p] for p in range(pieces)]

        def unpack(i, planes, arrived):
            return arrived.transpose(3, 1, 2, 0, 4, 5).reshape(sizes[i], 2, planes, edge, edge)

        return step(pack, unpack)

    return lax.cond(fits, send_sampled, send_all)


def finish(coil_groups, mine, full_slab, gradient, arrived, deep):
    edge = full_slab.shape[2]
    parts = edge // deep
    share = deep // coil_groups // len(arrived)
    rings = [[(i, (i + s) % coil_groups) for i in range(coil_groups)] for s in range(coil_groups)]
    pieces = [(p, p * coil_groups * share, share) for p in range(len(arrived))]
    if share % 2 == 0:
        p, first, _ = pieces.pop()
        pieces += [(p, first, share // 2), (p, first + coil_groups * share // 2, share // 2)]

    def start(p):
        one = gradient(p)
        mine_of = [piece for piece in pieces if piece[0] == p]
        leave = [
            [one(first + lax.rem(mine + s, coil_groups) * share, share, BF16) for s in range(1, coil_groups)]
            for _, first, share in mine_of
        ]
        away = [[lax.ppermute(term, "coil", ring) for term, ring in zip(terms, rings[1:])] for terms in leave]
        stay = [one(first + mine * share, share, F32, leave) for _, first, share in mine_of]
        return away, stay

    def to_cuts(i, away, summed):
        p, first, share = pieces[i]
        for term in away:
            summed = summed + term.astype(F32)
        base = lax.dynamic_slice_in_dim(full_slab, first + mine * share, share, 1).astype(F32)
        updated = (base - 0.5 * summed).astype(BF16)
        if p + 1 < len(arrived):
            updated, arrived[p + 1] = lax.optimization_barrier((updated, arrived[p + 1]))
        return lax.all_to_all(updated, "cuts", split_axis=2, concat_axis=1, tiled=True)

    def to_groups(updated):
        slab = updated.shape[2]
        share = updated.shape[1] // parts
        updated = updated.reshape(2, coil_groups, parts // coil_groups, share, slab, edge)
        whole = jnp.zeros((2, parts // coil_groups, coil_groups, share, slab, edge), BF16)
        for s in range(coil_groups):
            to = lax.rem(mine + s, coil_groups)
            source = lax.rem(mine + coil_groups - s, coil_groups)
            moved = lax.dynamic_index_in_dim(updated, to, 1, keepdims=False)
            if s:
                moved = lax.ppermute(moved, "coil", rings[s])
            whole = lax.dynamic_update_index_in_dim(whole, moved[:, :, None], source, 2)
        return whole.reshape(2, parts // coil_groups, coil_groups * share, slab, edge)

    out = []
    away, stay = start(0)
    for i, (p, _, _) in enumerate(pieces):
        updated = to_cuts(i, away.pop(0), stay.pop(0))
        if i + 1 < len(pieces):
            if not away:
                away, stay = start(p + 1)
            away[0], updated = lax.optimization_barrier((away[0], updated))
        out.append(to_groups(updated))
    out = jnp.concatenate(out, axis=2)
    return out.reshape(2, edge // coil_groups, out.shape[3], edge)


def solution(mesh):
    placed = (
        P(None, "cuts", "coil", None),
        P("coil", None, "cuts", None, None),
        P("coil", None, None, "cuts", None),
        P(),
    )
    return jax.shard_map(
        functools.partial(body, mesh.shape["coil"]),
        mesh=mesh,
        in_specs=placed,
        out_specs=P(None, "coil", "cuts", None),
        check_vma=False,
    )
```

```python
import functools
import math

import jax
import jax.numpy as jnp
from jax import lax
from jax.experimental import pallas as pl
from jax.experimental.pallas import tpu as pltpu
from jax.sharding import PartitionSpec as P

F32 = jnp.float32
BF16 = jnp.bfloat16
VMEM = 56 * 1024 * 1024
STEP = 2


def tables(length):
    counter = jnp.arange(length, dtype=jnp.int32)
    product = counter[:, None] * counter[None, :] % length
    angles = product.astype(jnp.float32) * (2.0 * math.pi / length)
    factor = 1.0 / math.sqrt(length)
    return (
        (jnp.cos(angles) * factor).astype(jnp.bfloat16),
        (jnp.sin(angles) * factor).astype(jnp.bfloat16),
    )


def dot(a, b):
    return lax.dot_general(a, b, (((1,), (0,)), ((), ())), preferred_element_type=F32)


def cost(flops, bytes_accessed):
    return pl.CostEstimate(flops=int(flops), bytes_accessed=int(bytes_accessed), transcendentals=0)


def layout_kernel(slab, mask_ref, place_ref, most_ref):
    edge = mask_ref.shape[1]
    half = edge // 2
    row = lax.broadcasted_iota(jnp.int32, (edge, edge), 0)
    column = lax.broadcasted_iota(jnp.int32, (edge, edge), 1)
    sampled = mask_ref[...] != 0

    def flags(where):
        return jnp.where(where, 1.0, 0.0).astype(BF16)

    rank = dot(flags(sampled), flags(row < column))
    over = jnp.maximum(dot(flags(sampled), flags(row >= 0)) - half, 0.0).astype(BF16)
    together = lax.div(row, slab) == lax.div(column, slab)
    before = dot(flags(together & (column < row)), over)
    most_ref[0] = jnp.max(dot(flags(together), over)).astype(jnp.int32)
    place = rank + jnp.where(rank < half, 0.0, before)
    place_ref[...] = jnp.where(sampled, place, -1.0).astype(jnp.int32)


def layout(line_mask, parts):
    lines, edge = line_mask.shape
    slab = lines // parts
    place, most = pl.pallas_call(
        functools.partial(layout_kernel, slab),
        out_specs=[pl.BlockSpec(memory_space=pltpu.VMEM), pl.BlockSpec(memory_space=pltpu.SMEM)],
        out_shape=[jax.ShapeDtypeStruct(line_mask.shape, jnp.int32), jax.ShapeDtypeStruct((1,), jnp.int32)],
        compiler_params=pltpu.CompilerParams(vmem_limit_bytes=VMEM),
        cost_estimate=cost(8 * edge**3, 8 * edge**2),
    )(line_mask)
    return most[0] <= edge // 2, place, edge // 2 * (slab + 1)


def compact_kernel(pieces, k_ref, s_ref, t_ref, *refs):
    out_refs, lines_ref, over_ref = refs[:pieces], refs[pieces], refs[pieces + 1]
    slab, _, edge = lines_ref.shape
    half = edge // 2
    parts, _, rows, _ = out_refs[0].shape
    step = 32

    @pl.loop(0, edge // step)
    def _(at):
        first = pl.multiple_of(at * step, step)
        for r in range(2):
            block = jnp.swapaxes(k_ref[0, r, pl.ds(first, step)], 0, 1)
            lines_ref[:, pl.ds(pl.multiple_of(r * edge + first, step), step), :] = block

    def send(picked, places):
        moved = dot(t_ref[...], picked.astype(BF16)).astype(BF16)
        moved = moved.reshape(parts, pieces, rows, picked.shape[1])
        for p in range(pieces):
            out_refs[p][:, 0, :, places] = moved[:, p]

    over_ref[...] = jnp.zeros_like(over_ref)

    @pl.loop(0, slab // 2)
    def _(pair):
        one = dot(lines_ref[2 * pair], s_ref[2 * pair])
        two = dot(lines_ref[2 * pair + 1], s_ref[2 * pair + 1])
        over_ref[...] += one[:, half:] + two[:, half:]
        own = jnp.concatenate([one[:, :half], two[:, :half]], axis=1)
        send(own, pl.ds(pl.multiple_of(pair * edge, edge), edge))

    send(over_ref[...], pl.ds(slab * half, half))


def by_destination(table, parts, pieces):
    size = table.shape[0]
    rows = table.reshape(2, parts, pieces, size // (2 * parts * pieces), size)
    return rows.transpose(1, 2, 0, 3, 4).reshape(size, size)


def compact(data, first_coil, coils, pieces, select, table, parts, slots):
    _, _, edge, slab, _ = data.shape
    rows = 2 * edge // parts // pieces
    return pl.pallas_call(
        functools.partial(compact_kernel, pieces),
        grid=(coils,),
        in_specs=[
            pl.BlockSpec((1, 2, edge, slab, edge), lambda c: (first_coil + c, 0, 0, 0, 0)),
            pl.BlockSpec(select.shape, lambda c: (0, 0, 0)),
            pl.BlockSpec(table.shape, lambda c: (0, 0)),
        ],
        out_specs=[pl.BlockSpec((parts, 1, rows, slots), lambda c: (0, c, 0, 0))] * pieces,
        out_shape=[jax.ShapeDtypeStruct((parts, coils, rows, slots), BF16)] * pieces,
        scratch_shapes=[pltpu.VMEM((slab, 2 * edge, edge), BF16), pltpu.VMEM((2 * edge, edge // 2), F32)],
        compiler_params=pltpu.CompilerParams(vmem_limit_bytes=VMEM),
        cost_estimate=cost(coils * 4 * slots * edge * 4 * edge, 4 * coils * edge * (slab * edge + slots)),
    )(data, select, by_destination(table, parts, pieces))


def expand_kernel(slab, place_ref, in_ref, out_ref, lines_ref):
    edge = place_ref.shape[1]
    half = edge // 2
    lines, rows, _ = lines_ref.shape
    places = lax.broadcasted_iota(jnp.int32, (edge, edge), 0)
    for k in range(lines):
        chosen = jnp.where(places == place_ref[k : k + 1, :], 1.0, 0.0).astype(BF16)
        at = k % slab * half
        own = in_ref[k // slab, :, :, at : at + half].reshape(rows, half)
        shared = in_ref[k // slab, :, :, slab * half :].reshape(rows, half)
        lines_ref[k] = dot(jnp.concatenate([own, shared], axis=1), chosen).astype(BF16)
    for at in range(0, rows, 16):
        out_ref[at : at + 16] = jnp.swapaxes(lines_ref[:, at : at + 16, :], 0, 1)


def expand(arrived, place):
    parts, coils, rows, slots = arrived.shape
    edge = place.shape[1]
    slab = place.shape[0] // parts
    rows = coils * rows
    slabs = STEP if parts % STEP == 0 else 1
    return pl.pallas_call(
        functools.partial(expand_kernel, slab),
        grid=(parts // slabs,),
        in_specs=[
            pl.BlockSpec((slabs * slab, edge), lambda d: (d, 0)),
            pl.BlockSpec((slabs,) + arrived.shape[1:], lambda d: (d, 0, 0, 0)),
        ],
        out_specs=pl.BlockSpec((rows, slabs * slab, edge), lambda d: (0, d, 0)),
        out_shape=jax.ShapeDtypeStruct((rows, parts * slab, edge), BF16),
        scratch_shapes=[pltpu.VMEM((slabs * slab, rows, edge), BF16)],
        compiler_params=pltpu.CompilerParams(vmem_limit_bytes=VMEM),
        cost_estimate=cost(parts * slab * rows * edge * edge * 2, 2 * (arrived.size + parts * slab * rows * edge)),
    )(place, arrived)


def forward_kernel(maps_ref, vol_ref, right_ref, left_ref, out_ref):
    edge = vol_ref.shape[3]
    for i in range(vol_ref.shape[1]):
        map_real, map_imag = maps_ref[0, 0, i].astype(F32), maps_ref[0, 1, i].astype(F32)
        vol_real, vol_imag = vol_ref[0, i].astype(F32), vol_ref[1, i].astype(F32)
        real = (map_real * vol_real - map_imag * vol_imag).astype(BF16)
        imag = (map_real * vol_imag + map_imag * vol_real).astype(BF16)
        along = dot(jnp.concatenate([real, imag], axis=1), right_ref[...]).astype(BF16)
        stacked = jnp.concatenate([along[:, :edge], along[:, edge:]], axis=0)
        out_ref[0, i] = dot(left_ref[...], stacked).astype(BF16)


def forward(maps, volume, right, left, group):
    coils, _, deep, edge, _ = maps.shape
    return pl.pallas_call(
        forward_kernel,
        grid=(deep // group, coils),
        in_specs=[
            pl.BlockSpec((1, 2, group, edge, edge), lambda x, c: (c, 0, x, 0, 0)),
            pl.BlockSpec((2, group, edge, edge), lambda x, c: (0, x, 0, 0)),
            pl.BlockSpec(right.shape, lambda x, c: (0, 0)),
            pl.BlockSpec(left.shape, lambda x, c: (0, 0)),
        ],
        out_specs=pl.BlockSpec((1, group, 2 * edge, edge), lambda x, c: (c, x, 0, 0)),
        out_shape=jax.ShapeDtypeStruct((coils, deep, 2 * edge, edge), BF16),
        compiler_params=pltpu.CompilerParams(vmem_limit_bytes=VMEM),
        cost_estimate=cost(coils * deep * edge**3 * 16, 4 * maps.size),
    )(maps, volume, right, left)


def backward_kernel(first, at_ref, *refs):
    if first:
        maps_ref, k_ref, h_ref, mask_ref, left_ref, right_ref, out_ref, sum_ref = refs
    else:
        maps_ref, k_ref, h_ref, mask_ref, left_ref, right_ref, before_ref, out_ref, sum_ref = refs
    edge = mask_ref.shape[1]
    sampled = mask_ref[...].astype(F32)
    sampled = jnp.concatenate([sampled, sampled], axis=0)

    @pl.when(pl.program_id(1) == 0)
    def _():
        sum_ref[...] = jnp.zeros_like(sum_ref) if first else before_ref[...]

    for i in range(k_ref.shape[1]):
        hybrid = h_ref[0, :, i].reshape(2 * edge, edge)
        residual = (sampled * (k_ref[0, i].astype(F32) - hybrid.astype(F32))).astype(BF16)
        back = dot(left_ref[...], residual).astype(BF16)
        back = jnp.concatenate([back[:edge], back[edge:]], axis=1)
        back = dot(back, right_ref[...]).astype(BF16).astype(F32)
        real, imag = back[:, :edge], back[:, edge:]
        map_real, map_imag = maps_ref[0, 0, i].astype(F32), maps_ref[0, 1, i].astype(F32)
        sum_ref[0, i] += map_real * real + map_imag * imag
        sum_ref[1, i] += map_real * imag - map_imag * real

    @pl.when(pl.program_id(1) == pl.num_programs(1) - 1)
    def _():
        out_ref[...] = sum_ref[...].astype(out_ref.dtype)


def backward(
    maps, coil_kspace, line_mask, left, right, group, hybrid, hybrid_x, before, first_coil, first_x, count, kind
):
    coils, _, _, edge, _ = hybrid.shape
    group = min(group, count)
    first = before is None
    block = (2, group, edge, edge)
    spec = pltpu.PrefetchScalarGridSpec(
        num_scalar_prefetch=1,
        grid=(count // group, coils),
        in_specs=[
            pl.BlockSpec((1, 2, group, edge, edge), lambda x, c, at: (first_coil + c, 0, at[0] + x, 0, 0)),
            pl.BlockSpec((1, group, 2 * edge, edge), lambda x, c, at: (first_coil + c, at[0] + x, 0, 0)),
            pl.BlockSpec((1, 2, group, edge, edge), lambda x, c, at: (c, 0, at[0] + x - hybrid_x // group, 0, 0)),
            pl.BlockSpec(line_mask.shape, lambda x, c, at: (0, 0)),
            pl.BlockSpec(left.shape, lambda x, c, at: (0, 0)),
            pl.BlockSpec(right.shape, lambda x, c, at: (0, 0)),
        ]
        + ([] if first else [pl.BlockSpec(block, lambda x, c, at: (0, at[0] + x, 0, 0))]),
        out_specs=pl.BlockSpec(block, lambda x, c, at: (0, x, 0, 0)),
        scratch_shapes=[pltpu.VMEM(block, F32)],
    )
    start = jnp.full((1,), first_x // group, jnp.int32)
    return pl.pallas_call(
        functools.partial(backward_kernel, first),
        grid_spec=spec,
        out_shape=jax.ShapeDtypeStruct((2, count, edge, edge), kind),
        compiler_params=pltpu.CompilerParams(vmem_limit_bytes=VMEM),
        cost_estimate=cost(coils * count * edge**3 * 16, count * edge**2 * (12 * coils + 16)),
    )(start, maps, coil_kspace, hybrid, line_mask, left, right, *([] if first else [before]))


def exchange(sent):
    return lax.all_to_all(sent, "cuts", split_axis=0, concat_axis=0, tiled=True)


def gather(coil_groups, mine, volume):
    planes, width = volume.shape[:2], volume.shape[2]
    whole = jnp.zeros(planes + (coil_groups * width, volume.shape[3]), BF16)
    for s in range(coil_groups):
        moved = volume
        if s:
            moved = lax.ppermute(volume, "coil", [(i, (i + s) % coil_groups) for i in range(coil_groups)])
        source = lax.rem(mine + coil_groups - s, coil_groups)
        whole = lax.dynamic_update_slice_in_dim(whole, moved, source * width, 2)
    return whole


def body(coil_groups, volume, coil_maps, kspace, line_mask):
    coils, _, deep, edge, _ = coil_maps.shape
    slab = kspace.shape[3]
    parts = edge // slab
    me = lax.axis_index("cuts")
    mine = lax.axis_index("coil")
    cos_table, sin_table = tables(edge)
    turn = jnp.block([[cos_table, sin_table], [-sin_table, cos_table]])
    turn_back = jnp.block([[cos_table, -sin_table], [sin_table, cos_table]])
    fits, place, slots = layout(line_mask, parts)
    if coils >= 6:
        sizes = [1, (coils - 3) // 2, (coils - 2) // 2, 2]
    else:
        sizes = [1] * coils
    firsts = [sum(sizes[:i]) for i in range(len(sizes))]
    pieces = min(2, deep // coil_groups)
    planes = deep // pieces
    last = len(sizes) - 1
    group = min(4, deep)

    def step(pack, unpack):
        full_slab = gather(coil_groups, mine, volume)
        arrived = []
        total = coil_kspace = None
        for i in range(last):
            (sent,) = pack(i, 1)
            if i == 1:
                sent, full_slab = lax.optimization_barrier((sent, full_slab))
                coil_kspace = forward(coil_maps, full_slab, turn_back, turn, group)
            elif i == 2:
                sent, coil_kspace = lax.optimization_barrier((sent, coil_kspace))
            arrived.append(exchange(sent))
        if coil_kspace is None:
            coil_kspace = forward(coil_maps, full_slab, turn_back, turn, group)
        back = functools.partial(backward, coil_maps, coil_kspace, line_mask, turn_back, turn, group)
        sent = list(pack(last, pieces))
        for i in range(last):
            if i == last - 1 and total is not None:
                sent[0], total = lax.optimization_barrier((sent[0], total))
            total = back(unpack(i, deep, arrived[i]), 0, total, firsts[i], 0, deep, F32)
        if pieces > 1:
            sent[1], total = lax.optimization_barrier((sent[1], total))
        arrived = [exchange(one) for one in sent]

        def gradient(p):
            hybrid = unpack(last, planes, arrived[p])

            def planes_from(first_x, count, kind, earlier=None):
                before = total
                if earlier is not None:
                    _, before = lax.optimization_barrier((earlier, total))
                return back(hybrid, p * planes, before, firsts[last], first_x, count, kind)

            return planes_from

        return finish(coil_groups, mine, full_slab, gradient, arrived, deep)

    def send_sampled():
        own = lax.dynamic_slice_in_dim(place, me * slab, slab, 0)
        select = (own[..., None] == jnp.arange(edge)).astype(BF16)

        def pack(i, pieces):
            return compact(kspace, firsts[i], sizes[i], pieces, select, turn_back, parts, slots)

        def unpack(i, planes, arrived):
            return expand(arrived, place).reshape(sizes[i], 2, planes, edge, edge)

        return step(pack, unpack)

    def send_all():
        def pack(i, pieces):
            part = lax.slice_in_dim(kspace, firsts[i], firsts[i] + sizes[i], axis=0)
            data = part.transpose(0, 3, 1, 2, 4).reshape(sizes[i], slab, 2 * edge, edge)
            table = by_destination(turn_back, parts, pieces)
            moved = jnp.einsum("xn,ckny->xcky", table, data, preferred_element_type=F32).astype(BF16)
            moved = moved.reshape(parts, pieces, 2, deep // pieces, sizes[i], slab, edge)
            return [moved[:, p] for p in range(pieces)]

        def unpack(i, planes, arrived):
            return arrived.transpose(3, 1, 2, 0, 4, 5).reshape(sizes[i], 2, planes, edge, edge)

        return step(pack, unpack)

    return lax.cond(fits, send_sampled, send_all)


def finish(coil_groups, mine, full_slab, gradient, arrived, deep):
    edge = full_slab.shape[2]
    parts = edge // deep
    share = deep // coil_groups // len(arrived)
    rings = [[(i, (i + s) % coil_groups) for i in range(coil_groups)] for s in range(coil_groups)]
    pieces = [(p, p * coil_groups * share, share) for p in range(len(arrived))]
    if share % 2 == 0:
        p, first, _ = pieces.pop()
        pieces += [(p, first, share // 2), (p, first + coil_groups * share // 2, share // 2)]

    def start(p):
        one = gradient(p)
        mine_of = [piece for piece in pieces if piece[0] == p]
        leave = [
            [one(first + lax.rem(mine + s, coil_groups) * share, share, BF16) for s in range(1, coil_groups)]
            for _, first, share in mine_of
        ]
        away = [[lax.ppermute(term, "coil", ring) for term, ring in zip(terms, rings[1:])] for terms in leave]
        stay = [one(first + mine * share, share, F32, leave) for _, first, share in mine_of]
        return away, stay

    def to_cuts(i, away, summed):
        p, first, share = pieces[i]
        for term in away:
            summed = summed + term.astype(F32)
        base = lax.dynamic_slice_in_dim(full_slab, first + mine * share, share, 1).astype(F32)
        updated = (base - 0.5 * summed).astype(BF16)
        updated = updated.reshape(2, share, parts, edge // parts, edge).transpose(2, 0, 1, 3, 4)
        if p + 1 < len(arrived):
            updated, arrived[p + 1] = lax.optimization_barrier((updated, arrived[p + 1]))
        return exchange(updated)

    def to_groups(updated):
        _, _, share, slab, _ = updated.shape
        updated = updated.reshape(coil_groups, parts // coil_groups, 2, share, slab, edge)
        whole = jnp.zeros((2, parts // coil_groups, coil_groups, share, slab, edge), BF16)
        for s in range(coil_groups):
            to = lax.rem(mine + s, coil_groups)
            source = lax.rem(mine + coil_groups - s, coil_groups)
            moved = lax.dynamic_index_in_dim(updated, to, 0, keepdims=False)
            if s:
                moved = lax.ppermute(moved, "coil", rings[s])
            moved = moved.transpose(1, 0, 2, 3, 4)[:, :, None]
            whole = lax.dynamic_update_index_in_dim(whole, moved, source, 2)
        return whole.reshape(2, parts // coil_groups, coil_groups * share, slab, edge)

    out = []
    away, stay = start(0)
    for i, (p, _, _) in enumerate(pieces):
        updated = to_cuts(i, away.pop(0), stay.pop(0))
        if i + 1 < len(pieces):
            if not away:
                away, stay = start(p + 1)
            away[0], updated = lax.optimization_barrier((away[0], updated))
        out.append(to_groups(updated))
    out = jnp.concatenate(out, axis=2)
    return out.reshape(2, edge // coil_groups, out.shape[3], edge)


def solution(mesh):
    placed = (
        P(None, "cuts", "coil", None),
        P("coil", None, "cuts", None, None),
        P("coil", None, None, "cuts", None),
        P(),
    )
    return jax.shard_map(
        functools.partial(body, mesh.shape["coil"]),
        mesh=mesh,
        in_specs=placed,
        out_specs=P(None, "coil", "cuts", None),
        check_vma=False,
    )
```

```python
import functools
import math

import jax
import jax.numpy as jnp
import numpy as np
from jax import lax
from jax.experimental import pallas as pl
from jax.experimental.pallas import tpu as pltpu
from jax.sharding import PartitionSpec as P

F32 = jnp.float32
BF16 = jnp.bfloat16
VMEM = 56 * 1024 * 1024
STEP = 2


def tables(length):
    counter = np.arange(length)
    angles = (counter[:, None] * counter[None, :] % length) * (2.0 * math.pi / length)
    factor = 1.0 / math.sqrt(length)
    return (np.cos(angles) * factor).astype(BF16), (np.sin(angles) * factor).astype(BF16)


def dot(a, b):
    return lax.dot_general(a, b, (((1,), (0,)), ((), ())), preferred_element_type=F32)


def cost(flops, bytes_accessed):
    return pl.CostEstimate(flops=int(flops), bytes_accessed=int(bytes_accessed), transcendentals=0)


def layout_kernel(slab, mask_ref, place_ref, most_ref):
    edge = mask_ref.shape[1]
    half = edge // 2
    row = lax.broadcasted_iota(jnp.int32, (edge, edge), 0)
    column = lax.broadcasted_iota(jnp.int32, (edge, edge), 1)
    sampled = mask_ref[...] != 0

    def flags(where):
        return jnp.where(where, 1.0, 0.0).astype(BF16)

    rank = dot(flags(sampled), flags(row < column))
    over = jnp.maximum(dot(flags(sampled), flags(row >= 0)) - half, 0.0).astype(BF16)
    together = lax.div(row, slab) == lax.div(column, slab)
    before = dot(flags(together & (column < row)), over)
    most_ref[0] = jnp.max(dot(flags(together), over)).astype(jnp.int32)
    place = rank + jnp.where(rank < half, 0.0, before)
    place_ref[...] = jnp.where(sampled, place, -1.0).astype(jnp.int32)


def layout(line_mask, parts):
    lines, edge = line_mask.shape
    slab = lines // parts
    place, most = pl.pallas_call(
        functools.partial(layout_kernel, slab),
        out_specs=[pl.BlockSpec(memory_space=pltpu.VMEM), pl.BlockSpec(memory_space=pltpu.SMEM)],
        out_shape=[jax.ShapeDtypeStruct(line_mask.shape, jnp.int32), jax.ShapeDtypeStruct((1,), jnp.int32)],
        compiler_params=pltpu.CompilerParams(vmem_limit_bytes=VMEM),
        cost_estimate=cost(8 * edge**3, 8 * edge**2),
    )(line_mask)
    return most[0] <= edge // 2, place, edge // 2 * (slab + 1)


def compact_kernel(pieces, k_ref, s_ref, t_ref, *refs):
    out_refs, lines_ref, over_ref = refs[:pieces], refs[pieces], refs[pieces + 1]
    slab, _, edge = lines_ref.shape
    half = edge // 2
    parts = out_refs[0].shape[0]
    step = 32

    @pl.loop(0, edge // step)
    def _(at):
        first = pl.multiple_of(at * step, step)
        for r in range(2):
            block = jnp.swapaxes(k_ref[0, r, pl.ds(first, step)], 0, 1)
            lines_ref[:, pl.ds(pl.multiple_of(r * edge + first, step), step), :] = block

    def send(picked, places):
        moved = dot(t_ref[...], picked.astype(BF16)).astype(BF16)
        moved = moved.reshape(parts, 2 * edge // parts, picked.shape[1])
        first = 0
        for out_ref in out_refs:
            rows = out_ref.shape[2]
            out_ref[:, 0, :, places] = moved[:, first : first + rows]
            first += rows

    over_ref[...] = jnp.zeros_like(over_ref)

    @pl.loop(0, slab // 2)
    def _(pair):
        one = dot(lines_ref[2 * pair], s_ref[2 * pair])
        two = dot(lines_ref[2 * pair + 1], s_ref[2 * pair + 1])
        over_ref[...] += one[:, half:] + two[:, half:]
        own = jnp.concatenate([one[:, :half], two[:, :half]], axis=1)
        send(own, pl.ds(pl.multiple_of(pair * edge, edge), edge))

    send(over_ref[...], pl.ds(slab * half, half))


def by_destination(table, parts, pieces):
    size = table.shape[0] // 2
    rows = np.arange(2 * size).reshape(2, parts, size // parts)
    cuts = np.split(rows, np.cumsum(pieces)[:-1], axis=2)
    order = [cut.transpose(1, 0, 2).reshape(parts, -1) for cut in cuts]
    return table[np.concatenate(order, axis=1).reshape(-1)]


def compact(data, first_coil, coils, pieces, select, table, parts, slots):
    _, _, edge, slab, _ = data.shape
    blocks = [(parts, 1, 2 * planes, slots) for planes in pieces]
    return pl.pallas_call(
        functools.partial(compact_kernel, len(pieces)),
        grid=(coils,),
        in_specs=[
            pl.BlockSpec((1, 2, edge, slab, edge), lambda c: (first_coil + c, 0, 0, 0, 0)),
            pl.BlockSpec(select.shape, lambda c: (0, 0, 0)),
            pl.BlockSpec(table.shape, lambda c: (0, 0)),
        ],
        out_specs=[pl.BlockSpec(block, lambda c: (0, c, 0, 0)) for block in blocks],
        out_shape=[jax.ShapeDtypeStruct((parts, coils) + block[2:], BF16) for block in blocks],
        scratch_shapes=[pltpu.VMEM((slab, 2 * edge, edge), BF16), pltpu.VMEM((2 * edge, edge // 2), F32)],
        compiler_params=pltpu.CompilerParams(vmem_limit_bytes=VMEM),
        cost_estimate=cost(coils * 4 * slots * edge * 4 * edge, 4 * coils * edge * (slab * edge + slots)),
    )(data, select, by_destination(table, parts, pieces))


def expand_kernel(slab, place_ref, in_ref, out_ref, lines_ref):
    edge = place_ref.shape[1]
    half = edge // 2
    lines, rows, _ = lines_ref.shape
    places = lax.broadcasted_iota(jnp.int32, (edge, edge), 0)
    for k in range(lines):
        chosen = jnp.where(places == place_ref[k : k + 1, :], 1.0, 0.0).astype(BF16)
        at = k % slab * half
        own = in_ref[k // slab, :, :, at : at + half].reshape(rows, half)
        shared = in_ref[k // slab, :, :, slab * half :].reshape(rows, half)
        lines_ref[k] = dot(jnp.concatenate([own, shared], axis=1), chosen).astype(BF16)
    for at in range(0, rows, 16):
        out_ref[at : at + 16] = jnp.swapaxes(lines_ref[:, at : at + 16, :], 0, 1)


def expand(arrived, place):
    parts, coils, rows, slots = arrived.shape
    edge = place.shape[1]
    slab = place.shape[0] // parts
    rows = coils * rows
    slabs = STEP if parts % STEP == 0 else 1
    return pl.pallas_call(
        functools.partial(expand_kernel, slab),
        grid=(parts // slabs,),
        in_specs=[
            pl.BlockSpec((slabs * slab, edge), lambda d: (d, 0)),
            pl.BlockSpec((slabs,) + arrived.shape[1:], lambda d: (d, 0, 0, 0)),
        ],
        out_specs=pl.BlockSpec((rows, slabs * slab, edge), lambda d: (0, d, 0)),
        out_shape=jax.ShapeDtypeStruct((rows, parts * slab, edge), BF16),
        scratch_shapes=[pltpu.VMEM((slabs * slab, rows, edge), BF16)],
        compiler_params=pltpu.CompilerParams(vmem_limit_bytes=VMEM),
        cost_estimate=cost(parts * slab * rows * edge * edge * 2, 2 * (arrived.size + parts * slab * rows * edge)),
    )(place, arrived)


def forward_kernel(maps_ref, vol_ref, right_ref, left_ref, out_ref):
    edge = vol_ref.shape[3]
    group = vol_ref.shape[1]
    rows = []
    for i in range(group):
        map_real, map_imag = maps_ref[0, 0, i].astype(F32), maps_ref[0, 1, i].astype(F32)
        vol_real, vol_imag = vol_ref[0, i].astype(F32), vol_ref[1, i].astype(F32)
        real = (map_real * vol_real - map_imag * vol_imag).astype(BF16)
        imag = (map_real * vol_imag + map_imag * vol_real).astype(BF16)
        rows.append(jnp.concatenate([real, imag], axis=1))
    planes = dot(jnp.concatenate(rows, axis=0), right_ref[...]).astype(BF16)
    for i in range(group):
        along = planes[i * edge : (i + 1) * edge]
        stacked = jnp.concatenate([along[:, :edge], along[:, edge:]], axis=0)
        out_ref[0, i] = dot(left_ref[...], stacked).astype(BF16)


def forward(maps, volume, right, left, group):
    coils, _, deep, edge, _ = maps.shape
    return pl.pallas_call(
        forward_kernel,
        grid=(deep // group, coils),
        in_specs=[
            pl.BlockSpec((1, 2, group, edge, edge), lambda x, c: (c, 0, x, 0, 0)),
            pl.BlockSpec((2, group, edge, edge), lambda x, c: (0, x, 0, 0)),
            pl.BlockSpec(right.shape, lambda x, c: (0, 0)),
            pl.BlockSpec(left.shape, lambda x, c: (0, 0)),
        ],
        out_specs=pl.BlockSpec((1, group, 2 * edge, edge), lambda x, c: (c, x, 0, 0)),
        out_shape=jax.ShapeDtypeStruct((coils, deep, 2 * edge, edge), BF16),
        compiler_params=pltpu.CompilerParams(vmem_limit_bytes=VMEM),
        cost_estimate=cost(coils * deep * edge**3 * 16, 4 * maps.size),
    )(maps, volume, right, left)


def backward_kernel(first, at_ref, *refs):
    if first:
        maps_ref, k_ref, h_ref, mask_ref, left_ref, right_ref, out_ref, sum_ref = refs
    else:
        maps_ref, k_ref, h_ref, mask_ref, left_ref, right_ref, before_ref, out_ref, sum_ref = refs
    edge = mask_ref.shape[1]
    sampled = mask_ref[...].astype(F32).astype(BF16)
    sampled = jnp.concatenate([sampled, sampled], axis=0)

    @pl.when(pl.program_id(1) == 0)
    def _():
        sum_ref[...] = jnp.zeros_like(sum_ref) if first else before_ref[...]

    group = k_ref.shape[1]
    rows = []
    for i in range(group):
        hybrid = h_ref[0, :, i].reshape(2 * edge, edge)
        residual = sampled * (k_ref[0, i] - hybrid)
        back = dot(left_ref[...], residual).astype(BF16)
        rows.append(jnp.concatenate([back[:edge], back[edge:]], axis=1))
    planes = dot(jnp.concatenate(rows, axis=0), right_ref[...]).astype(BF16)
    for i in range(group):
        back = planes[i * edge : (i + 1) * edge].astype(F32)
        real, imag = back[:, :edge], back[:, edge:]
        map_real, map_imag = maps_ref[0, 0, i].astype(F32), maps_ref[0, 1, i].astype(F32)
        sum_ref[0, i] += map_real * real + map_imag * imag
        sum_ref[1, i] += map_real * imag - map_imag * real

    @pl.when(pl.program_id(1) == pl.num_programs(1) - 1)
    def _():
        out_ref[...] = sum_ref[...].astype(out_ref.dtype)


def backward(
    maps,
    coil_kspace,
    line_mask,
    left,
    right,
    group,
    hybrid,
    hybrid_x,
    before,
    first_coil,
    first_x,
    count,
    kind,
):
    coils, _, _, edge, _ = hybrid.shape
    group = min(group, count)
    first = before is None
    block = (2, group, edge, edge)
    spec = pltpu.PrefetchScalarGridSpec(
        num_scalar_prefetch=1,
        grid=(count // group, coils),
        in_specs=[
            pl.BlockSpec((1, 2, group, edge, edge), lambda x, c, at: (first_coil + c, 0, at[0] + x, 0, 0)),
            pl.BlockSpec((1, group, 2 * edge, edge), lambda x, c, at: (first_coil + c, at[0] + x, 0, 0)),
            pl.BlockSpec((1, 2, group, edge, edge), lambda x, c, at: (c, 0, at[0] + x - hybrid_x // group, 0, 0)),
            pl.BlockSpec(line_mask.shape, lambda x, c, at: (0, 0)),
            pl.BlockSpec(left.shape, lambda x, c, at: (0, 0)),
            pl.BlockSpec(right.shape, lambda x, c, at: (0, 0)),
        ]
        + ([] if first else [pl.BlockSpec(block, lambda x, c, at: (0, at[0] + x, 0, 0))]),
        out_specs=pl.BlockSpec(block, lambda x, c, at: (0, x, 0, 0)),
        scratch_shapes=[pltpu.VMEM(block, F32)],
    )
    start = jnp.full((1,), first_x // group, jnp.int32)
    return pl.pallas_call(
        functools.partial(backward_kernel, first),
        grid_spec=spec,
        out_shape=jax.ShapeDtypeStruct((2, count, edge, edge), kind),
        compiler_params=pltpu.CompilerParams(vmem_limit_bytes=VMEM),
        cost_estimate=cost(coils * count * edge**3 * 16, count * edge**2 * (12 * coils + 16)),
    )(start, maps, coil_kspace, hybrid, line_mask, left, right, *([] if first else [before]))


def exchange(sent):
    return lax.all_to_all(sent, "cuts", split_axis=0, concat_axis=0, tiled=True)


def gather(coil_groups, mine, volume):
    planes, width = volume.shape[:2], volume.shape[2]
    whole = jnp.zeros(planes + (coil_groups * width, volume.shape[3]), BF16)
    for s in range(coil_groups):
        moved = volume
        if s:
            moved = lax.ppermute(volume, "coil", [(i, (i + s) % coil_groups) for i in range(coil_groups)])
        source = lax.rem(mine + coil_groups - s, coil_groups)
        whole = lax.dynamic_update_slice_in_dim(whole, moved, source * width, 2)
    return whole


def body(coil_groups, volume, coil_maps, kspace, line_mask):
    coils, _, deep, edge, _ = coil_maps.shape
    slab = kspace.shape[3]
    parts = edge // slab
    me = lax.axis_index("cuts")
    mine = lax.axis_index("coil")
    cos_table, sin_table = tables(edge)
    turn = np.block([[cos_table, sin_table], [-sin_table, cos_table]])
    turn_back = np.block([[cos_table, -sin_table], [sin_table, cos_table]])
    fits, place, slots = layout(line_mask, parts)
    if coils >= 8:
        sizes = [1, coils - 5, 4]
    else:
        sizes = [1] * coils
    firsts = [sum(sizes[:i]) for i in range(len(sizes))]
    quarter = deep // 4
    pieces = [3 * quarter, quarter] if deep % (4 * coil_groups) == 0 else [deep]
    last = len(sizes) - 1
    group = min(4, deep)

    def step(pack, unpack):
        full_slab = gather(coil_groups, mine, volume)
        arrived = []
        total = coil_kspace = None
        for i in range(last):
            (sent,) = pack(i, [deep])
            if i == 1:
                sent, full_slab = lax.optimization_barrier((sent, full_slab))
                coil_kspace = forward(coil_maps, full_slab, turn_back, turn, group)
            arrived.append(exchange(sent))
        if coil_kspace is None:
            coil_kspace = forward(coil_maps, full_slab, turn_back, turn, group)
        back = functools.partial(backward, coil_maps, coil_kspace, line_mask, turn_back, turn, group)
        sent = list(pack(last, pieces))
        for i in range(last):
            if i == last - 1 and total is not None:
                sent[0], total = lax.optimization_barrier((sent[0], total))
            hybrid = unpack(i, deep, arrived[i])
            total = back(hybrid, 0, total, firsts[i], 0, deep, F32)
        if len(pieces) > 1:
            sent[1], total = lax.optimization_barrier((sent[1], total))
        arrived = [exchange(one) for one in sent]

        def gradient(p):
            hybrid = unpack(last, pieces[p], arrived[p])

            def planes_from(first_x, count, kind, earlier=None):
                before = total
                if earlier is not None:
                    _, before = lax.optimization_barrier((earlier, total))
                return back(hybrid, sum(pieces[:p]), before, firsts[last], first_x, count, kind)

            return planes_from

        return finish(coil_groups, mine, full_slab, gradient, arrived, deep)

    def send_sampled():
        own = lax.dynamic_slice_in_dim(place, me * slab, slab, 0)
        select = (own[..., None] == jnp.arange(edge)).astype(BF16)

        def pack(i, pieces):
            return compact(kspace, firsts[i], sizes[i], pieces, select, turn_back, parts, slots)

        def unpack(i, planes, arrived):
            return expand(arrived, place).reshape(sizes[i], 2, planes, edge, edge)

        return step(pack, unpack)

    def send_all():
        def pack(i, pieces):
            part = lax.slice_in_dim(kspace, firsts[i], firsts[i] + sizes[i], axis=0)
            data = part.transpose(0, 3, 1, 2, 4).reshape(sizes[i], slab, 2 * edge, edge)
            table = by_destination(turn_back, parts, pieces)
            moved = jnp.einsum("xn,ckny->xcky", table, data, preferred_element_type=F32).astype(BF16)
            moved = moved.reshape(parts, 2 * deep, sizes[i], slab, edge)
            out = jnp.split(moved, [2 * sum(pieces[:p]) for p in range(1, len(pieces))], axis=1)
            return [one.reshape(parts, 2, one.shape[1] // 2, sizes[i], slab, edge) for one in out]

        def unpack(i, planes, arrived):
            return arrived.transpose(3, 1, 2, 0, 4, 5).reshape(sizes[i], 2, planes, edge, edge)

        return step(pack, unpack)

    return lax.cond(fits, send_sampled, send_all)


def finish(coil_groups, mine, full_slab, gradient, arrived, deep):
    edge = full_slab.shape[2]
    parts = edge // deep
    rings = [[(i, (i + s) % coil_groups) for i in range(coil_groups)] for s in range(coil_groups)]
    quarter = deep // coil_groups // 4
    if len(arrived) > 1:
        pieces = [(0, 0, 2 * quarter), (0, deep // 2, quarter), (1, deep * 3 // 4, quarter)]
    else:
        pieces = [(0, 0, deep // coil_groups)]

    def leave(p):
        one = gradient(p)
        return one, [
            [one(first + lax.rem(mine + s, coil_groups) * share, share, BF16) for s in range(1, coil_groups)]
            for at, first, share in pieces
            if at == p
        ]

    def send(terms):
        return [[lax.ppermute(term, "coil", ring) for term, ring in zip(piece, rings[1:])] for piece in terms]

    def stay(p, one, terms):
        return [one(first + mine * share, share, F32, terms) for at, first, share in pieces if at == p]

    def to_cuts(i, away, summed):
        p, first, share = pieces[i]
        for term in away:
            summed = summed + term.astype(F32)
        base = lax.dynamic_slice_in_dim(full_slab, first + mine * share, share, 1).astype(F32)
        updated = (base - 0.5 * summed).astype(BF16)
        updated = updated.reshape(2, share, parts, edge // parts, edge).transpose(2, 0, 1, 3, 4)
        if i == 0 and len(arrived) > 1:
            updated, arrived[p + 1] = lax.optimization_barrier((updated, arrived[p + 1]))
        return updated

    def to_groups(updated):
        _, _, share, slab, _ = updated.shape
        updated = updated.reshape(coil_groups, parts // coil_groups, 2, share, slab, edge)
        whole = jnp.zeros((2, parts // coil_groups, coil_groups, share, slab, edge), BF16)
        for s in range(coil_groups):
            to = lax.rem(mine + s, coil_groups)
            source = lax.rem(mine + coil_groups - s, coil_groups)
            moved = lax.dynamic_index_in_dim(updated, to, 0, keepdims=False)
            if s:
                moved = lax.ppermute(moved, "coil", rings[s])
            moved = moved.transpose(1, 0, 2, 3, 4)[:, :, None]
            whole = lax.dynamic_update_index_in_dim(whole, moved, source, 2)
        return whole.reshape(2, parts // coil_groups, coil_groups * share, slab, edge)

    out = []
    one, terms = leave(0)
    away, here = send(terms), stay(0, one, terms)
    for i, (p, _, _) in enumerate(pieces):
        updated = to_cuts(i, away.pop(0), here.pop(0))
        if i + 1 < len(pieces) and not away:
            one, terms = leave(p + 1)
            updated, terms = lax.optimization_barrier((updated, terms))
            away, here = send(terms), stay(p + 1, one, terms)
        updated = exchange(updated)
        if i + 1 < len(pieces):
            away[0], updated = lax.optimization_barrier((away[0], updated))
        out.append(to_groups(updated))
    out = jnp.concatenate(out, axis=2)
    return out.reshape(2, edge // coil_groups, out.shape[3], edge)


def solution(mesh):
    placed = (
        P(None, "cuts", "coil", None),
        P("coil", None, "cuts", None, None),
        P("coil", None, None, "cuts", None),
        P(),
    )
    return jax.shard_map(
        functools.partial(body, mesh.shape["coil"]),
        mesh=mesh,
        in_specs=placed,
        out_specs=P(None, "coil", "cuts", None),
        check_vma=False,
    )
```

```python
import functools
import math

import jax
import jax.numpy as jnp
import numpy as np
from jax import lax
from jax.experimental import pallas as pl
from jax.experimental.pallas import tpu as pltpu
from jax.sharding import PartitionSpec as P

F32 = jnp.float32
BF16 = jnp.bfloat16
VMEM = 56 * 1024 * 1024
STEP = 4


def tables(length):
    counter = np.arange(length)
    angles = (counter[:, None] * counter[None, :] % length) * (2.0 * math.pi / length)
    factor = 1.0 / math.sqrt(length)
    return (np.cos(angles) * factor).astype(BF16), (np.sin(angles) * factor).astype(BF16)


def dot(a, b):
    return lax.dot_general(a, b, (((1,), (0,)), ((), ())), preferred_element_type=F32)


def cost(flops, bytes_accessed):
    return pl.CostEstimate(flops=int(flops), bytes_accessed=int(bytes_accessed), transcendentals=0)


def layout_kernel(slab, mask_ref, place_ref, most_ref):
    edge = mask_ref.shape[1]
    half = edge // 2
    row = lax.broadcasted_iota(jnp.int32, (edge, edge), 0)
    column = lax.broadcasted_iota(jnp.int32, (edge, edge), 1)
    sampled = mask_ref[...] != 0

    def flags(where):
        return jnp.where(where, 1.0, 0.0).astype(BF16)

    rank = dot(flags(sampled), flags(row < column))
    over = jnp.maximum(dot(flags(sampled), flags(row >= 0)) - half, 0.0).astype(BF16)
    together = lax.div(row, slab) == lax.div(column, slab)
    before = dot(flags(together & (column < row)), over)
    most_ref[0] = jnp.max(dot(flags(together), over)).astype(jnp.int32)
    place = rank + jnp.where(rank < half, 0.0, before)
    place_ref[...] = jnp.where(sampled, place, -1.0).astype(jnp.int32)


def layout(line_mask, parts):
    lines, edge = line_mask.shape
    slab = lines // parts
    place, most = pl.pallas_call(
        functools.partial(layout_kernel, slab),
        out_specs=[pl.BlockSpec(memory_space=pltpu.VMEM), pl.BlockSpec(memory_space=pltpu.SMEM)],
        out_shape=[jax.ShapeDtypeStruct(line_mask.shape, jnp.int32), jax.ShapeDtypeStruct((1,), jnp.int32)],
        compiler_params=pltpu.CompilerParams(vmem_limit_bytes=VMEM),
        cost_estimate=cost(8 * edge**3, 8 * edge**2),
    )(line_mask)
    return most[0] <= edge // 2, place, edge // 2 * (slab + 1)


def compact_kernel(pieces, k_ref, s_ref, t_ref, *refs):
    out_refs, lines_ref, over_ref = refs[:pieces], refs[pieces], refs[pieces + 1]
    slab, _, edge = lines_ref.shape
    half = edge // 2
    parts = out_refs[0].shape[0]
    step = 32

    @pl.loop(0, edge // step)
    def _(at):
        first = pl.multiple_of(at * step, step)
        for r in range(2):
            block = jnp.swapaxes(k_ref[0, r, pl.ds(first, step)], 0, 1)
            lines_ref[:, pl.ds(pl.multiple_of(r * edge + first, step), step), :] = block

    def send(picked, places):
        moved = dot(t_ref[...], picked.astype(BF16)).astype(BF16)
        moved = moved.reshape(parts, 2 * edge // parts, picked.shape[1])
        first = 0
        for out_ref in out_refs:
            rows = out_ref.shape[2]
            out_ref[:, 0, :, places] = moved[:, first : first + rows]
            first += rows

    over_ref[...] = jnp.zeros_like(over_ref)

    @pl.loop(0, slab // 2)
    def _(pair):
        one = dot(lines_ref[2 * pair], s_ref[2 * pair])
        two = dot(lines_ref[2 * pair + 1], s_ref[2 * pair + 1])
        over_ref[...] += one[:, half:] + two[:, half:]
        own = jnp.concatenate([one[:, :half], two[:, :half]], axis=1)
        send(own, pl.ds(pl.multiple_of(pair * edge, edge), edge))

    send(over_ref[...], pl.ds(slab * half, half))


def by_destination(table, parts, pieces):
    size = table.shape[0] // 2
    rows = np.arange(2 * size).reshape(2, parts, size // parts)
    cuts = np.split(rows, np.cumsum(pieces)[:-1], axis=2)
    order = [cut.transpose(1, 0, 2).reshape(parts, -1) for cut in cuts]
    return table[np.concatenate(order, axis=1).reshape(-1)]


def compact(data, first_coil, coils, pieces, select, table, parts, slots):
    _, _, edge, slab, _ = data.shape
    blocks = [(parts, 1, 2 * planes, slots) for planes in pieces]
    return pl.pallas_call(
        functools.partial(compact_kernel, len(pieces)),
        grid=(coils,),
        in_specs=[
            pl.BlockSpec((1, 2, edge, slab, edge), lambda c: (first_coil + c, 0, 0, 0, 0)),
            pl.BlockSpec(select.shape, lambda c: (0, 0, 0)),
            pl.BlockSpec(table.shape, lambda c: (0, 0)),
        ],
        out_specs=[pl.BlockSpec(block, lambda c: (0, c, 0, 0)) for block in blocks],
        out_shape=[jax.ShapeDtypeStruct((parts, coils) + block[2:], BF16) for block in blocks],
        scratch_shapes=[pltpu.VMEM((slab, 2 * edge, edge), BF16), pltpu.VMEM((2 * edge, edge // 2), F32)],
        compiler_params=pltpu.CompilerParams(vmem_limit_bytes=VMEM),
        cost_estimate=cost(coils * 4 * slots * edge * 4 * edge, 4 * coils * edge * (slab * edge + slots)),
    )(data, select, by_destination(table, parts, pieces))


def expand_kernel(slab, place_ref, in_ref, out_ref, lines_ref):
    edge = place_ref.shape[1]
    half = edge // 2
    lines, rows, _ = lines_ref.shape
    places = lax.broadcasted_iota(jnp.int32, (edge, edge), 0)
    for k in range(lines):
        chosen = jnp.where(places == place_ref[k : k + 1, :], 1.0, 0.0).astype(BF16)
        at = k % slab * half
        own = in_ref[k // slab, :, :, at : at + half].reshape(rows, half)
        shared = in_ref[k // slab, :, :, slab * half :].reshape(rows, half)
        lines_ref[k] = dot(jnp.concatenate([own, shared], axis=1), chosen).astype(BF16)
    for at in range(0, rows, 16):
        out_ref[at : at + 16] = jnp.swapaxes(lines_ref[:, at : at + 16, :], 0, 1)


def expand(arrived, place):
    parts, coils, rows, slots = arrived.shape
    edge = place.shape[1]
    slab = place.shape[0] // parts
    rows = coils * rows
    slabs = STEP if parts % STEP == 0 else 1
    return pl.pallas_call(
        functools.partial(expand_kernel, slab),
        grid=(parts // slabs,),
        in_specs=[
            pl.BlockSpec((slabs * slab, edge), lambda d: (d, 0)),
            pl.BlockSpec((slabs,) + arrived.shape[1:], lambda d: (d, 0, 0, 0)),
        ],
        out_specs=pl.BlockSpec((rows, slabs * slab, edge), lambda d: (0, d, 0)),
        out_shape=jax.ShapeDtypeStruct((rows, parts * slab, edge), BF16),
        scratch_shapes=[pltpu.VMEM((slabs * slab, rows, edge), BF16)],
        compiler_params=pltpu.CompilerParams(vmem_limit_bytes=VMEM),
        cost_estimate=cost(parts * slab * rows * edge * edge * 2, 2 * (arrived.size + parts * slab * rows * edge)),
    )(place, arrived)


def forward_kernel(maps_ref, vol_ref, right_ref, left_ref, out_ref):
    edge = vol_ref.shape[3]
    group = vol_ref.shape[1]
    rows = []
    for i in range(group):
        map_real, map_imag = maps_ref[0, 0, i].astype(F32), maps_ref[0, 1, i].astype(F32)
        vol_real, vol_imag = vol_ref[0, i].astype(F32), vol_ref[1, i].astype(F32)
        real = (map_real * vol_real - map_imag * vol_imag).astype(BF16)
        imag = (map_real * vol_imag + map_imag * vol_real).astype(BF16)
        rows.append(jnp.concatenate([real, imag], axis=1))
    planes = dot(jnp.concatenate(rows, axis=0), right_ref[...]).astype(BF16)
    for i in range(group):
        along = planes[i * edge : (i + 1) * edge]
        stacked = jnp.concatenate([along[:, :edge], along[:, edge:]], axis=0)
        out_ref[0, i] = dot(left_ref[...], stacked).astype(BF16)


def forward(maps, volume, right, left, group):
    coils, _, deep, edge, _ = maps.shape
    return pl.pallas_call(
        forward_kernel,
        grid=(deep // group, coils),
        in_specs=[
            pl.BlockSpec((1, 2, group, edge, edge), lambda x, c: (c, 0, x, 0, 0)),
            pl.BlockSpec((2, group, edge, edge), lambda x, c: (0, x, 0, 0)),
            pl.BlockSpec(right.shape, lambda x, c: (0, 0)),
            pl.BlockSpec(left.shape, lambda x, c: (0, 0)),
        ],
        out_specs=pl.BlockSpec((1, group, 2 * edge, edge), lambda x, c: (c, x, 0, 0)),
        out_shape=jax.ShapeDtypeStruct((coils, deep, 2 * edge, edge), BF16),
        compiler_params=pltpu.CompilerParams(vmem_limit_bytes=VMEM),
        cost_estimate=cost(coils * deep * edge**3 * 16, 4 * maps.size),
    )(maps, volume, right, left)


def backward_kernel(first, at_ref, *refs):
    if first:
        maps_ref, k_ref, h_ref, mask_ref, left_ref, right_ref, out_ref, sum_ref = refs
    else:
        maps_ref, k_ref, h_ref, mask_ref, left_ref, right_ref, before_ref, out_ref, sum_ref = refs
    edge = mask_ref.shape[1]
    sampled = mask_ref[...].astype(F32).astype(BF16)
    sampled = jnp.concatenate([sampled, sampled], axis=0)

    @pl.when(pl.program_id(1) == 0)
    def _():
        sum_ref[...] = jnp.zeros_like(sum_ref) if first else before_ref[...]

    group = k_ref.shape[1]
    rows = []
    for i in range(group):
        hybrid = h_ref[0, :, i].reshape(2 * edge, edge)
        residual = sampled * (k_ref[0, i] - hybrid)
        back = dot(left_ref[...], residual).astype(BF16)
        rows.append(jnp.concatenate([back[:edge], back[edge:]], axis=1))
    planes = dot(jnp.concatenate(rows, axis=0), right_ref[...]).astype(BF16)
    for i in range(group):
        back = planes[i * edge : (i + 1) * edge].astype(F32)
        real, imag = back[:, :edge], back[:, edge:]
        map_real, map_imag = maps_ref[0, 0, i].astype(F32), maps_ref[0, 1, i].astype(F32)
        sum_ref[0, i] += map_real * real + map_imag * imag
        sum_ref[1, i] += map_real * imag - map_imag * real

    @pl.when(pl.program_id(1) == pl.num_programs(1) - 1)
    def _():
        out_ref[...] = sum_ref[...].astype(out_ref.dtype)


def backward(
    maps,
    coil_kspace,
    line_mask,
    left,
    right,
    group,
    hybrid,
    hybrid_x,
    before,
    first_coil,
    first_x,
    count,
    kind,
):
    coils, _, _, edge, _ = hybrid.shape
    group = min(group, count)
    first = before is None
    block = (2, group, edge, edge)
    spec = pltpu.PrefetchScalarGridSpec(
        num_scalar_prefetch=1,
        grid=(count // group, coils),
        in_specs=[
            pl.BlockSpec((1, 2, group, edge, edge), lambda x, c, at: (first_coil + c, 0, at[0] + x, 0, 0)),
            pl.BlockSpec((1, group, 2 * edge, edge), lambda x, c, at: (first_coil + c, at[0] + x, 0, 0)),
            pl.BlockSpec((1, 2, group, edge, edge), lambda x, c, at: (c, 0, at[0] + x - hybrid_x // group, 0, 0)),
            pl.BlockSpec(line_mask.shape, lambda x, c, at: (0, 0)),
            pl.BlockSpec(left.shape, lambda x, c, at: (0, 0)),
            pl.BlockSpec(right.shape, lambda x, c, at: (0, 0)),
        ]
        + ([] if first else [pl.BlockSpec(block, lambda x, c, at: (0, at[0] + x, 0, 0))]),
        out_specs=pl.BlockSpec(block, lambda x, c, at: (0, x, 0, 0)),
        scratch_shapes=[pltpu.VMEM(block, F32)],
    )
    start = jnp.full((1,), first_x // group, jnp.int32)
    return pl.pallas_call(
        functools.partial(backward_kernel, first),
        grid_spec=spec,
        out_shape=jax.ShapeDtypeStruct((2, count, edge, edge), kind),
        compiler_params=pltpu.CompilerParams(vmem_limit_bytes=VMEM),
        cost_estimate=cost(coils * count * edge**3 * 16, count * edge**2 * (12 * coils + 16)),
    )(start, maps, coil_kspace, hybrid, line_mask, left, right, *([] if first else [before]))


def exchange(sent):
    return lax.all_to_all(sent, "cuts", split_axis=0, concat_axis=0, tiled=True)


def gather(coil_groups, mine, volume):
    planes, width = volume.shape[:2], volume.shape[2]
    whole = jnp.zeros(planes + (coil_groups * width, volume.shape[3]), BF16)
    for s in range(coil_groups):
        moved = volume
        if s:
            moved = lax.ppermute(volume, "coil", [(i, (i + s) % coil_groups) for i in range(coil_groups)])
        source = lax.rem(mine + coil_groups - s, coil_groups)
        whole = lax.dynamic_update_slice_in_dim(whole, moved, source * width, 2)
    return whole


def body(coil_groups, volume, coil_maps, kspace, line_mask):
    coils, _, deep, edge, _ = coil_maps.shape
    slab = kspace.shape[3]
    parts = edge // slab
    me = lax.axis_index("cuts")
    mine = lax.axis_index("coil")
    cos_table, sin_table = tables(edge)
    turn = np.block([[cos_table, sin_table], [-sin_table, cos_table]])
    turn_back = np.block([[cos_table, -sin_table], [sin_table, cos_table]])
    fits, place, slots = layout(line_mask, parts)
    if coils >= 8:
        sizes = [1, coils - 5, 4]
    else:
        sizes = [1] * coils
    firsts = [sum(sizes[:i]) for i in range(len(sizes))]
    quarter = deep // 4
    pieces = [3 * quarter, quarter] if deep % (4 * coil_groups) == 0 else [deep]
    last = len(sizes) - 1
    group = min(4, deep)

    def step(pack, unpack):
        full_slab = gather(coil_groups, mine, volume)
        arrived = []
        total = coil_kspace = None
        for i in range(last):
            (sent,) = pack(i, [deep])
            if i == 1:
                sent, full_slab = lax.optimization_barrier((sent, full_slab))
                coil_kspace = forward(coil_maps, full_slab, turn_back, turn, group)
            arrived.append(exchange(sent))
        if coil_kspace is None:
            coil_kspace = forward(coil_maps, full_slab, turn_back, turn, group)
        back = functools.partial(backward, coil_maps, coil_kspace, line_mask, turn_back, turn, group)
        sent = list(pack(last, pieces))
        for i in range(last):
            if i == last - 1 and total is not None:
                sent[0], total = lax.optimization_barrier((sent[0], total))
            hybrid = unpack(i, deep, arrived[i])
            total = back(hybrid, 0, total, firsts[i], 0, deep, F32)
        if len(pieces) > 1:
            sent[1], total = lax.optimization_barrier((sent[1], total))
        arrived = [exchange(one) for one in sent]

        def gradient(p):
            hybrid = unpack(last, pieces[p], arrived[p])

            def planes_from(first_x, count, kind, earlier=None):
                before = total
                if earlier is not None:
                    _, before = lax.optimization_barrier((earlier, total))
                return back(hybrid, sum(pieces[:p]), before, firsts[last], first_x, count, kind)

            return planes_from

        return finish(coil_groups, mine, full_slab, gradient, arrived, deep)

    def send_sampled():
        own = lax.dynamic_slice_in_dim(place, me * slab, slab, 0)
        select = (own[..., None] == jnp.arange(edge)).astype(BF16)

        def pack(i, pieces):
            return compact(kspace, firsts[i], sizes[i], pieces, select, turn_back, parts, slots)

        def unpack(i, planes, arrived):
            return expand(arrived, place).reshape(sizes[i], 2, planes, edge, edge)

        return step(pack, unpack)

    def send_all():
        def pack(i, pieces):
            part = lax.slice_in_dim(kspace, firsts[i], firsts[i] + sizes[i], axis=0)
            data = part.transpose(0, 3, 1, 2, 4).reshape(sizes[i], slab, 2 * edge, edge)
            table = by_destination(turn_back, parts, pieces)
            moved = jnp.einsum("xn,ckny->xcky", table, data, preferred_element_type=F32).astype(BF16)
            moved = moved.reshape(parts, 2 * deep, sizes[i], slab, edge)
            out = jnp.split(moved, [2 * sum(pieces[:p]) for p in range(1, len(pieces))], axis=1)
            return [one.reshape(parts, 2, one.shape[1] // 2, sizes[i], slab, edge) for one in out]

        def unpack(i, planes, arrived):
            return arrived.transpose(3, 1, 2, 0, 4, 5).reshape(sizes[i], 2, planes, edge, edge)

        return step(pack, unpack)

    return lax.cond(fits, send_sampled, send_all)


def finish(coil_groups, mine, full_slab, gradient, arrived, deep):
    edge = full_slab.shape[2]
    parts = edge // deep
    rings = [[(i, (i + s) % coil_groups) for i in range(coil_groups)] for s in range(coil_groups)]
    quarter = deep // coil_groups // 4
    if len(arrived) > 1:
        pieces = [(0, 0, 2 * quarter), (0, deep // 2, quarter), (1, deep * 3 // 4, quarter)]
    else:
        pieces = [(0, 0, deep // coil_groups)]

    def leave(p):
        one = gradient(p)
        return one, [
            [one(first + lax.rem(mine + s, coil_groups) * share, share, BF16) for s in range(1, coil_groups)]
            for at, first, share in pieces
            if at == p
        ]

    def send(terms):
        return [[lax.ppermute(term, "coil", ring) for term, ring in zip(piece, rings[1:])] for piece in terms]

    def stay(p, one, terms):
        return [one(first + mine * share, share, F32, terms) for at, first, share in pieces if at == p]

    def to_cuts(i, away, summed):
        p, first, share = pieces[i]
        for term in away:
            summed = summed + term.astype(F32)
        base = lax.dynamic_slice_in_dim(full_slab, first + mine * share, share, 1).astype(F32)
        updated = (base - 0.5 * summed).astype(BF16)
        updated = updated.reshape(2, share, parts, edge // parts, edge).transpose(2, 0, 1, 3, 4)
        if i == 0 and len(arrived) > 1:
            updated, arrived[p + 1] = lax.optimization_barrier((updated, arrived[p + 1]))
        return updated

    def to_groups(updated):
        _, _, share, slab, _ = updated.shape
        updated = updated.reshape(coil_groups, parts // coil_groups, 2, share, slab, edge)
        whole = jnp.zeros((2, parts // coil_groups, coil_groups, share, slab, edge), BF16)
        for s in range(coil_groups):
            to = lax.rem(mine + s, coil_groups)
            source = lax.rem(mine + coil_groups - s, coil_groups)
            moved = lax.dynamic_index_in_dim(updated, to, 0, keepdims=False)
            if s:
                moved = lax.ppermute(moved, "coil", rings[s])
            moved = moved.transpose(1, 0, 2, 3, 4)[:, :, None]
            whole = lax.dynamic_update_index_in_dim(whole, moved, source, 2)
        return whole.reshape(2, parts // coil_groups, coil_groups * share, slab, edge)

    out = []
    one, terms = leave(0)
    away, here = send(terms), stay(0, one, terms)
    for i, (p, _, _) in enumerate(pieces):
        updated = to_cuts(i, away.pop(0), here.pop(0))
        if i + 1 < len(pieces) and not away:
            one, terms = leave(p + 1)
            updated, terms = lax.optimization_barrier((updated, terms))
            away, here = send(terms), stay(p + 1, one, terms)
        updated = exchange(updated)
        if i + 1 < len(pieces):
            away[0], updated = lax.optimization_barrier((away[0], updated))
        out.append(to_groups(updated))
    out = jnp.concatenate(out, axis=2)
    return out.reshape(2, edge // coil_groups, out.shape[3], edge)


def solution(mesh):
    placed = (
        P(None, "cuts", "coil", None),
        P("coil", None, "cuts", None, None),
        P("coil", None, None, "cuts", None),
        P(),
    )
    return jax.shard_map(
        functools.partial(body, mesh.shape["coil"]),
        mesh=mesh,
        in_specs=placed,
        out_specs=P(None, "coil", "cuts", None),
        check_vma=False,
    )
```
